512 devices in a mesh: shard: 64 (over x, y, core), rep: 8 (over z).
Axes of the slice: x: 4, y: 8, z: 8, core: 2. Of those that a mesh axis runs over, the one named last changes fastest.
Arguments:
- hidden_acts: bfloat16 [8, 16384, 128], P('rep', 'shard'), may hold values from -6 to 6
- out_grads: bfloat16 [8, 16384, 6144], P('rep', 'shard'), may hold values from -16 to 16
- momentum: float32 [8, 192, 4096], P('rep', 'shard'), may hold values from -6 to 6
- weight_tiles: bfloat16 [192, 4096], P('shard'), may hold values from -1.5 to 1.5
- kept_ids: int32 [8, 192, 4], P('rep', 'shard'), may hold values from 0 to 31, as said below
- kept_counts: int32 [8, 192], P('rep', 'shard'), may hold values from 1 to 4, as said below
Outputs:
- weight_next: bfloat16 [192, 4096], replicated
- momentum_next: float32 [8, 192, 4096], P('rep', 'shard')
The draws below stay inside these ranges and needn't reach their ends.
Inputs may be any that keep to these rules, and one draw needn't show every extreme that they name: `kept_ids`: the 4 block numbers of one replica's tile are distinct. `kept_counts`: every replica keeps all 4 blocks in at least one tile.
All inputs are finite; a program needn't handle non-finite values.
Results may differ from the reference program's by a relative error of at most 0.007.
Values may be sent and summed in bfloat16 or wider, within the bound.
A program may use at most 64 MiB of HBM per device.

```python
import math
import jax
import jax.numpy as jnp
from jax import lax

D = 6144
ROWS = 128
TILE = 64
BROWS = 8
BCOLS = 16
KEPT = 4
BLOCKS = 32
TILE_SQ = 4096
TILES = 192
TOK_GROUP = 16384
REPS = 8


def draw_kept_ids(key, part):
    key = jax.random.fold_in(key, 11)
    scores = jax.random.randint(key, (REPS, TILES, BLOCKS), 0, 1 << 20) * BLOCKS
    scores = scores + jnp.arange(BLOCKS).astype(jnp.int32)[None, None, :]
    ranked = jnp.argsort(scores, axis=-1)
    return ranked[:, :, :KEPT].astype(jnp.int32)


def draw_kept_counts(key, part):
    key = jax.random.fold_in(key, 12)
    first_key, second_key = jax.random.split(key)
    base_counts = jax.random.randint(first_key, (REPS, TILES), 1, KEPT + 1)
    full_tile = jax.random.randint(second_key, (REPS, 1), 0, TILES)
    tile_index = jnp.arange(TILES).astype(jnp.int32)[None, :]
    return jnp.where(tile_index == full_tile, KEPT, base_counts).astype(jnp.int32)


def raised(drawn, rng, source, target, shards_of, factor):
    def block_of(dim):
        return (jnp.arange(drawn.shape[dim]) // (drawn.shape[dim] // shards_of)).reshape((-1,) + (1,) * (drawn.ndim - 1 - dim))

    one_side = jax.random.permutation(rng, shards_of)[block_of(target)]
    other_side = (block_of(target) + shards_of // 2) % shards_of
    return jnp.where((block_of(source) == one_side) | (block_of(source) == other_side), factor * drawn, drawn)


def shard_levels(key, dims, pieces, low, largest):
    def one(axis_at, blocks):
        heights = jax.random.uniform(jax.random.fold_in(jax.random.fold_in(key, 6), axis_at), (blocks,), jnp.float32, low / len(pieces), largest / len(pieces))
        return jnp.repeat(jnp.exp(heights), dims[axis_at] // blocks).reshape((-1,) + (1,) * (len(dims) - axis_at - 1))

    gain = one(*pieces[0])
    for cut in pieces[1:]:
        gain = gain * one(*cut)
    return gain


def centred(key, shape, scale, limit, pieces=(), held_as=jnp.bfloat16):
    level = shard_levels(key, shape, pieces, -0.22, 0.18) if pieces else 1.0
    drawn = jax.random.normal(key, shape, jnp.float32) * scale * level
    return jnp.minimum(jnp.maximum(drawn, -limit), limit).astype(held_as)


def gaussian_with(key, shape, scale, bound, pieces, heavy, kind=jnp.bfloat16):
    drawn = scale * jax.random.normal(key, shape, jnp.float32)
    if pieces:
        drawn = drawn * shard_levels(key, shape, pieces, -0.22, 0.18)
    return jnp.clip(raised(drawn, jax.random.fold_in(key, 3), *heavy), -bound, bound).astype(kind)


def setup_inputs(seed: int = 0) -> dict:
    arg_keys = jax.random.split(jax.random.key(seed), 7)
    hidden_acts = centred(arg_keys[0], (REPS, TOK_GROUP, ROWS), 1.0, 6.0, ((0, 8), (1, 64)))
    out_grads = gaussian_with(arg_keys[1], (REPS, TOK_GROUP, D), 1.0, 16.0, ((0, 8), (1, 64)), (1, 2, 64, 4.0))
    momentum = centred(arg_keys[2], (REPS, TILES, TILE_SQ), 1.0, 6.0, ((0, 8), (1, 64)), jnp.float32)
    weight_tiles = centred(arg_keys[3], (TILES, TILE_SQ), 0.25, 1.5, ((0, 64),))
    kept_ids = draw_kept_ids(jax.random.fold_in(arg_keys[6], 71), 0)
    kept_counts = draw_kept_counts(jax.random.fold_in(arg_keys[6], 71), 0)
    return {"hidden_acts": hidden_acts, "out_grads": out_grads, "momentum": momentum, "weight_tiles": weight_tiles, "kept_ids": kept_ids, "kept_counts": kept_counts}


MOMENTUM_DECAY = 0.9
STEP_FACTOR = 2.0
PRECISE = lax.Precision.HIGHEST

def cosine_basis(basis_order):
    freq_rows = jnp.arange(basis_order).astype(jnp.float32)[:, None]
    sample_cols = jnp.arange(basis_order).astype(jnp.float32)[None, :]
    raw_basis = jnp.cos(math.pi * (2.0 * sample_cols + 1.0) * freq_rows / (2.0 * basis_order))
    norm_scale = jnp.where(freq_rows == 0.0, math.sqrt(1.0 / basis_order), math.sqrt(2.0 / basis_order))
    return raw_basis * norm_scale

def to_tiles(grad_mat, tile_size):
    row_count, mat_width = grad_mat.shape
    shaped = grad_mat.reshape(row_count // tile_size, tile_size, mat_width // tile_size, tile_size)
    return shaped.transpose(0, 2, 1, 3).reshape(-1, tile_size * tile_size)

def slot_hits(block_ids, block_counts, block_total):
    slot_count = block_ids.shape[-1]
    live_slot = jnp.arange(slot_count).astype(jnp.int32)[None, :] < block_counts[:, None]
    match_block = block_ids[:, :, None] == jnp.arange(block_total).astype(jnp.int32)[None, None, :]
    return jnp.where(live_slot[:, :, None] & match_block, 1.0, 0.0).astype(jnp.float32)

def expand_blocks(keep_mask, tile_size, block_rows, block_cols):
    lead_count = keep_mask.shape[0]
    block_grid = keep_mask.reshape(lead_count, tile_size // block_rows, 1, tile_size // block_cols, 1)
    full_grid = jnp.broadcast_to(block_grid, (lead_count, tile_size // block_rows, block_rows, tile_size // block_cols, block_cols))
    return full_grid.reshape(lead_count, tile_size, tile_size)

def reference(hidden_acts, out_grads, momentum, weight_tiles, kept_ids, kept_counts):
    cos_basis = cosine_basis(TILE)
    grad_scale = 1.0 / math.sqrt(TOK_GROUP)

    def one_replica(inputs):
        hidden_rows, grad_out, moment_old, block_ids, block_counts = inputs
        grad_mat = jnp.dot(hidden_rows.T, grad_out, preferred_element_type=jnp.float32) * grad_scale
        moment_new = MOMENTUM_DECAY * moment_old + to_tiles(grad_mat, TILE)
        moment_new = moment_new.reshape(TILES, TILE, TILE)
        coeffs = jnp.einsum('ab,nbc,dc->nad', cos_basis, moment_new, cos_basis, precision=PRECISE)
        keep_mask = lax.optimization_barrier(jnp.sum(slot_hits(block_ids, block_counts, BLOCKS), axis=1))
        kept_coef = coeffs * expand_blocks(keep_mask, TILE, BROWS, BCOLS)
        moment_out = moment_new - jnp.einsum('ba,nbc,cd->nad', cos_basis, kept_coef, cos_basis, precision=PRECISE)
        return (moment_out.reshape(TILES, TILE_SQ), kept_coef.astype(jnp.bfloat16))
    moment_out, sent_coef = lax.map(one_replica, (hidden_acts, out_grads, momentum, kept_ids, kept_counts))
    coef_total = lax.optimization_barrier(jnp.sum(sent_coef.astype(jnp.float32), axis=0))
    update = jnp.einsum('ba,nbc,cd->nad', cos_basis, coef_total, cos_basis, precision=PRECISE).reshape(TILES, TILE_SQ)
    weight_next = (weight_tiles.astype(jnp.float32) - STEP_FACTOR / REPS * update).astype(jnp.bfloat16)
    return (weight_next, moment_out)
```

```python
import math

import jax
import jax.numpy as jnp
import numpy as np
from jax import lax
from jax.experimental import pallas as pl
from jax.experimental.pallas import tpu as pltpu
from jax.sharding import PartitionSpec as P

TILE = 64
BLOCKS = 32
TILE_SQ = 4096
D = 6144
NX, NY, NZ = 4, 8, 8
ROWS = 96
HALF = 48
PARTS = 4
PART_COLS = D // PARTS
PART_CHIPS = PART_COLS // 384
MOMENTUM_DECAY = 0.9
STEP = 2.0 / 8.0
GRAD_SCALE = 1.0 / 128.0
MESH = pl.DeviceIdType.MESH
F32 = jnp.float32
BF16 = jnp.bfloat16


def constants():
    k = np.arange(TILE, dtype=np.float64)[:, None]
    n = np.arange(TILE, dtype=np.float64)[None, :]
    basis = np.cos(math.pi * (2 * n + 1) * k / (2 * TILE))
    basis *= np.where(k == 0, math.sqrt(1 / TILE), math.sqrt(2 / TILE))
    even, odd = basis[:, 0::2], basis[:, 1::2]
    out = np.zeros((448, 128))
    out[0:128] = np.tile(basis.T, (2, 2))
    out[128:192, 0:64] = basis
    out[192:256, 64:128] = basis
    out[256:384, 0:32] = np.concatenate([even, odd], 0)
    out[384:448, 0:64] = np.concatenate([even.T, odd.T], 0)
    return out.astype(np.float32)


def dot32(a, b):
    return lax.dot_general(
        a, b, (((1,), (0,)), ((), ())), precision=lax.Precision.HIGHEST, preferred_element_type=F32
    )


def iota(shape, dim):
    return lax.broadcasted_iota(jnp.int32, shape, dim)


def kernel(
    hid, grads, mom, wts, ids, counts, consts,
    gath, mom_out,
    gbuf, part, prx, msum, wsum, zbuf, acc, slab,
    s0h, s0f, r0h, r0f, t0h, t0f, u0h, u0f,
    s1h, s1f, r1h, r1f, t1h, t1f, u1h, u1f,
    s2h, s2f, r2h, r2f, t2h, t2f, u2h, u2f,
    load_sem, pair_s, pair_r, rs_s, rs_r, z_s, z_r, ag_s, ag_r, fw_s, fw_r,
):
    shard, z = lax.axis_index("shard"), lax.axis_index("rep")
    c = shard % 2
    y = (shard // 2) % NY
    x = shard // (2 * NY)

    def dev(xx, yy, cc):
        return ((xx * NY + yy) * 2 + cc, z)

    pair = dev(x, y, 1 - c)

    loads = []
    for p in range(PARTS):
        cp = pltpu.make_async_copy(
            grads.at[0, :, pl.ds(p * PART_COLS, PART_COLS)], gbuf.at[p], load_sem.at[p]
        )
        cp.start()
        loads.append(cp)

    barrier = pltpu.get_barrier_semaphore()
    partners = [pair]
    for d in (1, NX - 1):
        partners.append(dev((x + d) % NX, y, c))
    for d in (1, NY - 1):
        partners.append(dev(x, (y + d) % NY, c))
    for d in range(1, NZ):
        partners.append((shard, (z + d) % NZ))
    for who in partners:
        pl.semaphore_signal(barrier, inc=1, device_id=who, device_id_type=MESH)

    r_, c_ = iota((128, 128), 0), iota((128, 128), 1)
    src = (r_ // 64) * 64 + (r_ % 32) * 2 + (r_ % 64) // 32
    perm = jnp.where(c_ == src, 1.0, 0.0).astype(BF16)
    hid_t = lax.dot_general(
        perm, hid[0], (((1,), (1,)), ((), ())), preferred_element_type=F32
    ).astype(BF16)

    for m in range(32):
        msum[pl.ds(m, 3, stride=32), :] = mom[0, :, m * 128:(m + 1) * 128]
        wsum[pl.ds(m, 3, stride=32), :] = wts[:, m * 128:(m + 1) * 128].astype(F32)

    left = iota((32, 128), 1) < 64
    pair_copies = []
    for p in range(PARTS):
        loads[p].wait()
        full = jnp.dot(hid_t, gbuf[p], preferred_element_type=F32)
        for i in range(2):
            for q in range(PART_CHIPS):
                chip = i * 16 + p * PART_CHIPS + q
                for b in range(3):
                    cols = slice(q * 384 + b * 128, q * 384 + (b + 1) * 128)
                    ev = full[i * 64:i * 64 + 32, cols]
                    od = full[i * 64 + 32:i * 64 + 64, cols]
                    first = jnp.where(left, ev, pltpu.roll(od, 64, 1)).astype(BF16)
                    second = jnp.where(left, pltpu.roll(ev, 64, 1), od).astype(BF16)
                    for t, val in ((2 * b, first), (2 * b + 1, second)):
                        row = (t % 3) * 32
                        part[t // 3, chip // 8, chip % 8, row:row + 32, :] = val
        if p == 0:
            pl.semaphore_wait(barrier, len(partners))
        for i in range(2):
            lo = (i * 16 + p * PART_CHIPS) // 8
            yy = (p * PART_CHIPS) % 8
            cp = pltpu.make_async_remote_copy(
                src_ref=part.at[1 - c, lo, pl.ds(yy, PART_CHIPS)],
                dst_ref=prx.at[lo, pl.ds(yy, PART_CHIPS)],
                send_sem=pair_s.at[p * 2 + i],
                recv_sem=pair_r.at[p * 2 + i],
                device_id=pair,
                device_id_type=MESH,
            )
            cp.start()
            pair_copies.append(cp)
    for cp in pair_copies:
        cp.wait()

    def ring_reduce(n, pos, who, local, bufs, base):
        sh, sf, rh, rf, th, tf, uh, uf = bufs
        h = n // 2
        copies = []
        prev = None
        for t in range(h):
            o = h - t
            right, lft = (pos + o) % n, (pos + n - o) % n
            if t == 0:
                sh[...] = local(right, 0, HALF).astype(BF16)
                th[...] = local(lft, HALF, ROWS).astype(BF16)
                pairs = ((sh, rh), (th, uh))
            else:
                a, b = sf.at[t - 1], tf.at[t - 1]
                if t == 1:
                    a[..., 0:HALF, :] = (local(right, 0, HALF) + rh[...].astype(F32)).astype(BF16)
                    a[..., HALF:ROWS, :] = local(right, HALF, ROWS).astype(BF16)
                    b[..., 0:HALF, :] = local(lft, 0, HALF).astype(BF16)
                    b[..., HALF:ROWS, :] = (local(lft, HALF, ROWS) + uh[...].astype(F32)).astype(BF16)
                else:
                    a[...] = (local(right, 0, ROWS) + rf[t - 2].astype(F32)).astype(BF16)
                    b[...] = (local(lft, 0, ROWS) + uf[t - 2].astype(F32)).astype(BF16)
                pairs = ((a, rf.at[t - 1]), (b, uf.at[t - 1]))
            now = []
            for k, (s, r) in enumerate(pairs):
                cp = pltpu.make_async_remote_copy(
                    src_ref=s, dst_ref=r,
                    send_sem=rs_s.at[base + 2 * t + k], recv_sem=rs_r.at[base + 2 * t + k],
                    device_id=who((pos + (1 if k == 0 else n - 1)) % n), device_id_type=MESH,
                )
                cp.start()
                now.append(cp)
            for cp in now:
                cp.wait_recv()
            copies += now
        total = local(pos, 0, ROWS) + rf[h - 2].astype(F32) + uf[h - 2].astype(F32)
        for cp in copies:
            cp.wait_send()
        return total

    def own(ix):
        return part[(c,) + ix].astype(F32) + prx[ix].astype(F32)

    y_of = lambda v: dev(x, v, c)
    x_of = lambda v: dev(v, y, c)
    bufs0 = (s0h, s0f, r0h, r0f, t0h, t0f, u0h, u0f)
    bufs1 = (s1h, s1f, r1h, r1f, t1h, t1f, u1h, u1f)

    bufs2 = (s2h, s2f, r2h, r2f, t2h, t2f, u2h, u2f)

    def summed(v, lo, hi):
        return acc[v, lo:hi]

    @pl.when(c == 0)
    def _():
        acc[0:NX] = ring_reduce(
            NY, y, y_of, lambda v, lo, hi: own((slice(None), v, slice(lo, hi))), bufs0, 0
        )
        slab[...] = ring_reduce(NX, x, x_of, summed, bufs2, 8)

    @pl.when(c == 1)
    def _():
        acc[...] = ring_reduce(
            NX, x, x_of, lambda v, lo, hi: own((v, slice(None), slice(lo, hi))), bufs1, 0
        )
        slab[...] = ring_reduce(NY, y, y_of, summed, bufs2, 4)

    moment = MOMENTUM_DECAY * msum[...] + GRAD_SCALE * slab[...]
    both, diag = consts[0:128], consts[128:256]
    fwd, inv = consts[256:384, 0:32], consts[384:448, 0:64]
    tiles = jnp.concatenate([moment[0:32], moment[32:64], moment[64:96]], axis=1)
    v = dot32(fwd, tiles)
    left64 = iota((64, 128), 1) < 64
    v = jnp.concatenate(
        [
            jnp.where(left64, v[0:64, k * 128:(k + 1) * 128], v[64:128, k * 128:(k + 1) * 128])
            for k in range(3)
        ],
        axis=0,
    )
    coef = dot32(v, both)

    group = (iota((64, 128), 1) % 64) // 16
    unit = (iota((64, 128), 0) // 8) * 4 + group
    kept = []
    for k in range(3):
        keep = jnp.zeros((64, 128), F32)
        for j in range(4):
            live = jnp.where(j < counts[0, k], ids[0, k, j], -1)
            keep = jnp.where(unit == live, 1.0, keep)
        kept.append(coef[k * 64:(k + 1) * 64] * keep)

    lane8 = iota((8, 128), 1)
    row8 = iota((8, 128), 0)
    picked = []
    numbers = jnp.zeros((8, 128), F32)
    for k in range(3):
        for j in range(4):
            number = ids[0, k, j]
            block = jnp.zeros((8, 128), F32)
            for p in range(8):
                block = jnp.where(number // 4 == p, kept[k][p * 8:(p + 1) * 8], block)
            here = (lane8 // 16) == number % 4
            picked.append(jnp.where(here & (j < counts[0, k]), block, 0.0))
            slot = (row8 == k) & (lane8 // 16 == 4 + j)
            numbers = jnp.where(slot, number.astype(F32), numbers)
    picked = jnp.concatenate(picked, axis=0).astype(BF16)
    spread = jnp.where(
        iota((128, 128), 0) % 16 == iota((128, 128), 1) % 16, 1.0, 0.0
    ).astype(BF16)
    picked = jnp.dot(picked, spread, preferred_element_type=F32)
    halves = [jnp.zeros((8, 128), F32), numbers]
    for k in range(3):
        for j in range(4):
            at = (k * 4 + j) * 8
            halves[k // 2] = jnp.where(
                lane8 // 16 == (k % 2) * 4 + j, picked[at:at + 8], halves[k // 2]
            )
    zbuf[z] = jnp.concatenate(halves, axis=0).astype(BF16)
    sends = []
    for d in range(1, NZ):
        cp = pltpu.make_async_remote_copy(
            src_ref=zbuf.at[z], dst_ref=zbuf.at[z],
            send_sem=z_s.at[d - 1], recv_sem=z_r.at[d - 1],
            device_id=(shard, (z + d) % NZ), device_id_type=MESH,
        )
        cp.start()
        sends.append(cp)

    def inverse(rows):
        kb = dot32(rows, diag)
        kb = jnp.concatenate([kb[0:64], kb[64:128], kb[128:192]], axis=1)
        w = dot32(inv, kb)
        return jnp.concatenate(
            [
                jnp.where(left, w[0:32, k * 128:(k + 1) * 128], w[32:64, k * 128:(k + 1) * 128])
                for k in range(3)
            ],
            axis=0,
        )

    msum[...] = moment - inverse(jnp.concatenate(kept, axis=0))
    for m in range(32):
        mom_out[0, :, m * 128:(m + 1) * 128] = msum[pl.ds(m, 3, stride=32), :]

    for d in range(1, NZ):
        frm = (z + NZ - d) % NZ
        pltpu.make_async_remote_copy(
            src_ref=zbuf.at[z], dst_ref=zbuf.at[frm],
            send_sem=z_s.at[d - 1], recv_sem=z_r.at[d - 1],
            device_id=(shard, frm), device_id_type=MESH,
        ).wait_recv()

    wide = iota((128, 1024), 1)
    pick = (wide // 128 == iota((128, 1024), 0) // 16) & (wide % 16 == iota((128, 1024), 0) % 16)
    pick = jnp.where(pick, 1.0, 0.0).astype(BF16)
    msgs = jnp.concatenate([zbuf[r] for r in range(NZ)], axis=0)
    vals = jnp.dot(msgs, pick, preferred_element_type=F32)
    unitf = unit.astype(F32)
    totals = []
    for k in range(3):
        total = jnp.zeros((64, 128), F32)
        for r in range(NZ):
            for j in range(4):
                col = ((k % 2) * 4 + j) * 128
                row = r * 16 + (k // 2) * 8
                val = vals[row:row + 8, col:col + 128]
                num = vals[r * 16 + 8 + k:r * 16 + 9 + k, (4 + j) * 128:(5 + j) * 128]
                val = jnp.concatenate([val] * 8, axis=0)
                total = total + jnp.where(unitf == num, val, 0.0)
        totals.append(total)
    update = inverse(jnp.concatenate(totals, axis=0))
    gath[x, y, c] = (wsum[...] - STEP * update).astype(BF16)

    def hand_on(chunk, k):
        return pltpu.make_async_remote_copy(
            src_ref=chunk, dst_ref=chunk, send_sem=fw_s.at[k], recv_sem=fw_r.at[k],
            device_id=pair, device_id_type=MESH,
        )

    def ring_gather(n, pos, who, chunk, base, arrived):
        h = n // 2
        copies = []
        for t in range(1, h + 1):
            lo, hi = ((0, HALF), (HALF, ROWS)) if t == h else ((0, ROWS), (0, ROWS))
            now = []
            for k, (at, to, rows) in enumerate((
                ((pos + n - (t - 1)) % n, (pos + 1) % n, lo), ((pos + t - 1) % n, (pos + n - 1) % n, hi)
            )):
                ref = chunk(at, *rows)
                cp = pltpu.make_async_remote_copy(
                    src_ref=ref, dst_ref=ref,
                    send_sem=ag_s.at[base + 2 * (t - 1) + k], recv_sem=ag_r.at[base + 2 * (t - 1) + k],
                    device_id=who(to), device_id_type=MESH,
                )
                cp.start()
                now.append(cp)
            for k, (cp, at, rows) in enumerate(
                zip(now, ((pos + n - t) % n, (pos + t) % n), (lo, hi))
            ):
                ref = chunk(at, *rows)
                pltpu.make_async_remote_copy(
                    src_ref=ref, dst_ref=ref,
                    send_sem=ag_s.at[base + 2 * (t - 1) + k], recv_sem=ag_r.at[base + 2 * (t - 1) + k],
                    device_id=pair, device_id_type=MESH,
                ).wait_recv()
                if arrived is not None:
                    arrived(at, rows, 2 * (t - 1) + k + 1)
            copies += now
        for cp in copies:
            cp.wait_send()

    def column(cc):
        return lambda v, lo=0, hi=ROWS: gath.at[:, v, cc, pl.ds(lo, hi - lo)]

    def line(cc):
        return lambda v, lo=0, hi=ROWS: gath.at[v, :, cc, pl.ds(lo, hi - lo)]

    def one_x(v, lo, hi):
        return gath.at[v, y, c, pl.ds(lo, hi - lo)]

    def one_y(v, lo, hi):
        return gath.at[x, v, c, pl.ds(lo, hi - lo)]

    def passed_on(n, pos, chunk):
        out = [hand_on(chunk(pos), 0)]
        for t in range(1, n // 2 + 1):
            lo, hi = ((0, HALF), (HALF, ROWS)) if t == n // 2 else ((0, ROWS), (0, ROWS))
            out.append(hand_on(chunk((pos + n - t) % n, *lo), 2 * t - 1))
            out.append(hand_on(chunk((pos + t) % n, *hi), 2 * t))
        return out

    def finish(n, pos, who, chunk, base, other_n, other_pos, other_chunk):
        mine = passed_on(n, pos, chunk)
        mine[0].start()
        ring_gather(n, pos, who, chunk, base, lambda at, rows, k: mine[k].start())
        for cp in passed_on(other_n, other_pos, other_chunk):
            cp.wait_recv()
        for cp in mine:
            cp.wait_send()

    @pl.when(c == 0)
    def _():
        ring_gather(NX, x, x_of, one_x, 8, None)
        finish(NY, y, y_of, column(0), 0, NX, x, line(1))

    @pl.when(c == 1)
    def _():
        ring_gather(NY, y, y_of, one_y, 4, None)
        finish(NX, x, x_of, line(1), 0, NY, y, column(0))

    for cp in sends:
        cp.wait_send()


def body(hidden_acts, out_grads, momentum, weight_tiles, kept_ids, kept_counts):
    vmem = pl.BlockSpec(memory_space=pltpu.VMEM)
    smem = pl.BlockSpec(memory_space=pltpu.SMEM)

    def ring_bufs(lead, steps):
        half = pltpu.VMEM(lead + (HALF, 128), BF16)
        whole = pltpu.VMEM((steps,) + lead + (ROWS, 128), BF16)
        return [half, whole] * 4

    dma = pltpu.SemaphoreType.DMA
    gathered, moment_out = pl.pallas_call(
        kernel,
        out_shape=(
            jax.ShapeDtypeStruct((NX, NY, 2, ROWS, 128), BF16),
            jax.ShapeDtypeStruct((1, 3, TILE_SQ), F32),
        ),
        in_specs=[vmem, pl.BlockSpec(memory_space=pl.ANY), vmem, vmem, smem, smem, vmem],
        out_specs=(vmem, vmem),
        scratch_shapes=[
            pltpu.VMEM((PARTS, 256, PART_COLS), BF16),
            pltpu.VMEM((2, NX, NY, ROWS, 128), BF16),
            pltpu.VMEM((NX, NY, ROWS, 128), BF16),
            pltpu.VMEM((ROWS, 128), F32),
            pltpu.VMEM((ROWS, 128), F32),
            pltpu.VMEM((NZ, 16, 128), BF16),
            pltpu.VMEM((NY, ROWS, 128), F32),
            pltpu.VMEM((ROWS, 128), F32),
            *ring_bufs((NX,), 3),
            *ring_bufs((NY,), 1),
            *ring_bufs((), 3),
            dma((PARTS,)),
            dma((2 * PARTS,)),
            dma((2 * PARTS,)),
            dma((12,)),
            dma((12,)),
            dma((NZ - 1,)),
            dma((NZ - 1,)),
            dma((12,)),
            dma((12,)),
            dma((9,)),
            dma((9,)),
        ],
        compiler_params=pltpu.CompilerParams(
            collective_id=0, has_side_effects=True, vmem_limit_bytes=48 * 1024 * 1024
        ),
    )(
        hidden_acts, out_grads, momentum, weight_tiles, kept_ids, kept_counts, jnp.asarray(constants())
    )
    return gathered.reshape(192, TILE_SQ), moment_out


def solution(mesh):
    in_specs = (
        P("rep", "shard", None),
        P("rep", "shard", None),
        P("rep", "shard", None),
        P("shard", None),
        P("rep", "shard", None),
        P("rep", "shard"),
    )
    out_specs = (P(), P("rep", "shard", None))
    return jax.shard_map(body, mesh=mesh, in_specs=in_specs, out_specs=out_specs, check_vma=False)
```

```python
import math

import jax
import jax.numpy as jnp
import numpy as np
from jax import lax
from jax.experimental import pallas as pl
from jax.experimental.pallas import tpu as pltpu
from jax.sharding import PartitionSpec as P

TILE = 64
BLOCKS = 32
TILE_SQ = 4096
D = 6144
NX, NY, NZ = 4, 8, 8
ROWS = 96
Y_ROWS = 32
G_ROWS = 32
X_NEAR = (1, 3, 2)
Y_NEAR = (1, 7, 2, 6, 3, 5, 4)
PARTS = 4
PART_COLS = D // PARTS
PART_CHIPS = PART_COLS // 384
BARRIER_AT = 3
MOMENTUM_DECAY = 0.9
STEP = 2.0 / 8.0
GRAD_SCALE = 1.0 / 128.0
MESH = pl.DeviceIdType.MESH
F32 = jnp.float32
BF16 = jnp.bfloat16


def constants():
    k = np.arange(TILE, dtype=np.float64)[:, None]
    n = np.arange(TILE, dtype=np.float64)[None, :]
    basis = np.cos(math.pi * (2 * n + 1) * k / (2 * TILE))
    basis *= np.where(k == 0, math.sqrt(1 / TILE), math.sqrt(2 / TILE))
    even, odd = basis[:, 0::2], basis[:, 1::2]
    out = np.zeros((448, 128))
    out[0:128] = np.tile(basis.T, (2, 2))
    out[128:192, 0:64] = basis
    out[192:256, 64:128] = basis
    out[256:384, 0:32] = np.concatenate([even, odd], 0)
    out[384:448, 0:64] = np.concatenate([even.T, odd.T], 0)
    return out.astype(np.float32)


def dot32(a, b):
    return lax.dot_general(
        a, b, (((1,), (0,)), ((), ())), precision=lax.Precision.HIGHEST, preferred_element_type=F32
    )


def iota(shape, dim):
    return lax.broadcasted_iota(jnp.int32, shape, dim)


def kernel(
    hid, grads, mom, wts, ids, counts, consts,
    gath, mom_out,
    hid_v, gbuf, mom_v, wts_v, ids_v, counts_v, consts_v,
    part, prx, wsum, zbuf, slab, acc_y, acc_x,
    st_y1, rx_y1, st_x1, rx_x1, st_y2, rx_y2, st_x2, rx_x2,
    load_sem, in_sem, pair_s, pair_r,
    y1_s, y1_r, x1_s, x1_r, y2_s, y2_r, x2_s, x2_r,
    z_s, z_r, gy_s, gy_r, gx_s, gx_r, ry_s, ry_r, rx_s, rx_r, fw_s, fw_r,
):
    shard, z = lax.axis_index("shard"), lax.axis_index("rep")
    c = shard % 2
    y = (shard // 2) % NY
    x = shard // (2 * NY)

    def dev(xx, yy, cc):
        return ((xx * NY + yy) * 2 + cc, z)

    def y_at(d):
        return (y + d) % NY

    def x_at(d):
        return (x + d) % NX

    def to_y(d):
        return dev(x, y_at(d), c)

    def to_x(d):
        return dev(x_at(d), y, c)

    def remote(src, dst, send, recv, who):
        return pltpu.make_async_remote_copy(
            src_ref=src, dst_ref=dst, send_sem=send, recv_sem=recv,
            device_id=who, device_id_type=MESH,
        )

    pair = dev(x, y, 1 - c)
    barrier = pltpu.get_barrier_semaphore()
    partners = [pair] + [to_x(d) for d in X_NEAR] + [to_y(d) for d in Y_NEAR]
    partners += [(shard, (z + d) % NZ) for d in range(1, NZ)]
    for who in partners:
        pl.semaphore_signal(barrier, inc=1, device_id=who, device_id_type=MESH)

    moves = []
    for k, (src, dst) in enumerate((
        (hid.at[0], hid_v), (mom, mom_v), (wts, wts_v), (ids, ids_v), (counts, counts_v),
        (consts, consts_v),
    )):
        moves.append(pltpu.make_async_copy(src, dst, in_sem.at[k]))
    moves[0].start()
    loads = []
    for p in range(PARTS):
        cp = pltpu.make_async_copy(
            grads.at[0, :, pl.ds(p * PART_COLS, PART_COLS)], gbuf.at[p], load_sem.at[p]
        )
        cp.start()
        loads.append(cp)
    for cp in moves[1:]:
        cp.start()
    moves[0].wait()

    r_, c_ = iota((128, 128), 0), iota((128, 128), 1)
    src = (r_ // 64) * 64 + (r_ % 32) * 2 + (r_ % 64) // 32
    perm = jnp.where(c_ == src, 1.0, 0.0).astype(BF16)
    hid_t = lax.dot_general(
        perm, hid_v[...], (((1,), (1,)), ((), ())), preferred_element_type=F32
    ).astype(BF16)

    left = iota((32, 128), 1) < 64
    pair_copies = []
    for p in range(PARTS):
        loads[p].wait()
        full = jnp.dot(hid_t, gbuf[p], preferred_element_type=F32)
        for i in range(2):
            for q in range(PART_CHIPS):
                chip = i * 16 + p * PART_CHIPS + q
                for b in range(3):
                    cols = slice(q * 384 + b * 128, q * 384 + (b + 1) * 128)
                    ev = full[i * 64:i * 64 + 32, cols]
                    od = full[i * 64 + 32:i * 64 + 64, cols]
                    first = jnp.where(left, ev, pltpu.roll(od, 64, 1)).astype(BF16)
                    second = jnp.where(left, pltpu.roll(ev, 64, 1), od).astype(BF16)
                    for t, val in ((2 * b, first), (2 * b + 1, second)):
                        row = (t % 3) * 32
                        part[t // 3, chip // 8, chip % 8, row:row + 32, :] = val
        if p == BARRIER_AT:
            pl.semaphore_wait(barrier, len(partners))
        for i in range(2):
            lo = (i * 16 + p * PART_CHIPS) // 8
            yy = (p * PART_CHIPS) % 8
            cp = pltpu.make_async_remote_copy(
                src_ref=part.at[1 - c, lo, pl.ds(yy, PART_CHIPS)],
                dst_ref=prx.at[lo, pl.ds(yy, PART_CHIPS)],
                send_sem=pair_s.at[p * 2 + i],
                recv_sem=pair_r.at[p * 2 + i],
                device_id=pair,
                device_id_type=MESH,
            )
            pair_copies.append(cp)
        if p >= BARRIER_AT:
            for cp in pair_copies[0 if p == BARRIER_AT else -2:]:
                cp.start()
    for cp in pair_copies:
        cp.wait()


    def own(ix):
        return part[(c,) + ix].astype(F32) + prx[ix].astype(F32)

    ys, xs = slice(0, Y_ROWS), slice(Y_ROWS, ROWS)
    every = slice(None)
    first_x, first_y, second_y, second_x = [], [], [], []
    for d in X_NEAR:
        st_x1[d - 1] = own((x_at(d), every, xs)).astype(BF16)
        cp = remote(st_x1.at[d - 1], rx_x1.at[d - 1], x1_s.at[d - 1], x1_r.at[d - 1], to_x(d))
        cp.start()
        first_x.append(cp)
    for d in Y_NEAR:
        st_y1[d - 1] = own((every, y_at(d), ys)).astype(BF16)
        cp = remote(st_y1.at[d - 1], rx_y1.at[d - 1], y1_s.at[d - 1], y1_r.at[d - 1], to_y(d))
        cp.start()
        first_y.append(cp)
    total = own((x, every, xs))
    for cp, d in zip(first_x, X_NEAR):
        cp.wait_recv()
        total = total + rx_x1[d - 1].astype(F32)
    acc_x[...] = total
    for d in Y_NEAR:
        st_y2[d - 1] = acc_x[y_at(d)].astype(BF16)
        cp = remote(st_y2.at[d - 1], rx_y2.at[d - 1], y2_s.at[d - 1], y2_r.at[d - 1], to_y(d))
        cp.start()
        second_y.append(cp)
    total = own((every, y, ys))
    for cp, d in zip(first_y, Y_NEAR):
        cp.wait_recv()
        total = total + rx_y1[d - 1].astype(F32)
    acc_y[...] = total
    for d in X_NEAR:
        st_x2[d - 1] = acc_y[x_at(d)].astype(BF16)
        cp = remote(st_x2.at[d - 1], rx_x2.at[d - 1], x2_s.at[d - 1], x2_r.at[d - 1], to_x(d))
        cp.start()
        second_x.append(cp)
    total = acc_x[y]
    for cp, d in zip(second_y, Y_NEAR):
        cp.wait_recv()
        total = total + rx_y2[d - 1].astype(F32)
    slab[xs] = total
    total = acc_y[x]
    for cp, d in zip(second_x, X_NEAR):
        cp.wait_recv()
        total = total + rx_x2[d - 1].astype(F32)
    slab[ys] = total
    for cp in moves[1:]:
        cp.wait()

    moment = MOMENTUM_DECAY * mom_v[...] + GRAD_SCALE * slab[...]
    both, diag = consts_v[0:128], consts_v[128:256]
    fwd, inv = consts_v[256:384, 0:32], consts_v[384:448, 0:64]
    tiles = jnp.concatenate([moment[0:32], moment[32:64], moment[64:96]], axis=1)
    v = dot32(fwd, tiles)
    left64 = iota((64, 128), 1) < 64
    v = jnp.concatenate(
        [
            jnp.where(left64, v[0:64, k * 128:(k + 1) * 128], v[64:128, k * 128:(k + 1) * 128])
            for k in range(3)
        ],
        axis=0,
    )
    coef = dot32(v, both)

    group = (iota((64, 128), 1) % 64) // 16
    unit = (iota((64, 128), 0) // 8) * 4 + group
    kept = []
    for k in range(3):
        keep = jnp.zeros((64, 128), F32)
        for j in range(4):
            live = jnp.where(j < counts_v[0, k], ids_v[k, 0, j], -1)
            keep = jnp.where(unit == live, 1.0, keep)
        kept.append(coef[k * 64:(k + 1) * 64] * keep)

    lane8 = iota((8, 128), 1)
    row8 = iota((8, 128), 0)
    picked = []
    numbers = jnp.zeros((8, 128), F32)
    for k in range(3):
        for j in range(4):
            number = ids_v[k, 0, j]
            block = jnp.zeros((8, 128), F32)
            for p in range(8):
                block = jnp.where(number // 4 == p, kept[k][p * 8:(p + 1) * 8], block)
            here = (lane8 // 16) == number % 4
            picked.append(jnp.where(here & (j < counts_v[0, k]), block, 0.0))
            slot = (row8 == k) & (lane8 // 16 == 4 + j)
            numbers = jnp.where(slot, number.astype(F32), numbers)
    picked = jnp.concatenate(picked, axis=0).astype(BF16)
    spread = jnp.where(
        iota((128, 128), 0) % 16 == iota((128, 128), 1) % 16, 1.0, 0.0
    ).astype(BF16)
    picked = jnp.dot(picked, spread, preferred_element_type=F32)
    halves = [jnp.zeros((8, 128), F32), numbers]
    for k in range(3):
        for j in range(4):
            at = (k * 4 + j) * 8
            halves[k // 2] = jnp.where(
                lane8 // 16 == (k % 2) * 4 + j, picked[at:at + 8], halves[k // 2]
            )
    zbuf[z] = jnp.concatenate(halves, axis=0).astype(BF16)
    sends = []
    for d in range(1, NZ):
        cp = pltpu.make_async_remote_copy(
            src_ref=zbuf.at[z], dst_ref=zbuf.at[z],
            send_sem=z_s.at[d - 1], recv_sem=z_r.at[d - 1],
            device_id=(shard, (z + d) % NZ), device_id_type=MESH,
        )
        cp.start()
        sends.append(cp)

    def inverse(rows):
        kb = dot32(rows, diag)
        kb = jnp.concatenate([kb[0:64], kb[64:128], kb[128:192]], axis=1)
        w = dot32(inv, kb)
        return jnp.concatenate(
            [
                jnp.where(left, w[0:32, k * 128:(k + 1) * 128], w[32:64, k * 128:(k + 1) * 128])
                for k in range(3)
            ],
            axis=0,
        )

    mom_out[...] = moment - inverse(jnp.concatenate(kept, axis=0))
    for m in range(32):
        wsum[pl.ds(m, 3, stride=32), :] = wts_v[:, m * 128:(m + 1) * 128].astype(F32)

    for d in range(1, NZ):
        frm = (z + NZ - d) % NZ
        pltpu.make_async_remote_copy(
            src_ref=zbuf.at[z], dst_ref=zbuf.at[frm],
            send_sem=z_s.at[d - 1], recv_sem=z_r.at[d - 1],
            device_id=(shard, frm), device_id_type=MESH,
        ).wait_recv()

    wide = iota((128, 1024), 1)
    pick = (wide // 128 == iota((128, 1024), 0) // 16) & (wide % 16 == iota((128, 1024), 0) % 16)
    pick = jnp.where(pick, 1.0, 0.0).astype(BF16)
    msgs = jnp.concatenate([zbuf[r] for r in range(NZ)], axis=0)
    vals = jnp.dot(msgs, pick, preferred_element_type=F32)
    unitf = unit.astype(F32)
    totals = []
    for k in range(3):
        total = jnp.zeros((64, 128), F32)
        for r in range(NZ):
            for j in range(4):
                col = ((k % 2) * 4 + j) * 128
                row = r * 16 + (k // 2) * 8
                val = vals[row:row + 8, col:col + 128]
                num = vals[r * 16 + 8 + k:r * 16 + 9 + k, (4 + j) * 128:(5 + j) * 128]
                val = jnp.concatenate([val] * 8, axis=0)
                total = total + jnp.where(unitf == num, val, 0.0)
        totals.append(total)
    update = inverse(jnp.concatenate(totals, axis=0))
    gath[x, y, c] = (wsum[...] - STEP * update).astype(BF16)


    sends += first_x + first_y + second_x + second_y
    lower, upper = pl.ds(0, G_ROWS), pl.ds(G_ROWS, ROWS - G_ROWS)

    def same(ref, send, recv, who):
        return remote(ref, ref, send, recv, who)

    mine = gath.at[x, y, c]
    for d in X_NEAR:
        cp = same(mine, gx_s.at[d - 1], gx_r.at[d - 1], to_x(d))
        cp.start()
        sends.append(cp)
    for d in Y_NEAR:
        cp = same(mine, gy_s.at[d - 1], gy_r.at[d - 1], to_y(d))
        cp.start()
        sends.append(cp)

    def hand_on(cc, dx, dy):
        k = dx * NY + dy
        return same(gath.at[x_at(NX - dx), y_at(NY - dy), cc], fw_s.at[k], fw_r.at[k], pair)

    def give(dx, dy):
        cp = hand_on(c, dx, dy)
        cp.start()
        sends.append(cp)

    give(0, 0)
    for dx in X_NEAR:
        src = gath.at[x_at(NX - dx), y, c]
        same(src, gx_s.at[dx - 1], gx_r.at[dx - 1], pair).wait_recv()
        for dy in Y_NEAR:
            k = (dx - 1) * 7 + dy - 1
            cp = same(src.at[lower], ry_s.at[k], ry_r.at[k], to_y(dy))
            cp.start()
            sends.append(cp)
        give(dx, 0)
    for dy in Y_NEAR:
        src = gath.at[x, y_at(NY - dy), c]
        same(src, gy_s.at[dy - 1], gy_r.at[dy - 1], pair).wait_recv()
        for dx in X_NEAR:
            k = (dx - 1) * 7 + dy - 1
            cp = same(src.at[upper], rx_s.at[k], rx_r.at[k], to_x(dx))
            cp.start()
            sends.append(cp)
        give(0, dy)
    for dy in Y_NEAR:
        for dx in X_NEAR:
            k = (dx - 1) * 7 + dy - 1
            dst = gath.at[x_at(NX - dx), y_at(NY - dy), c]
            same(dst.at[lower], ry_s.at[k], ry_r.at[k], pair).wait_recv()
            same(dst.at[upper], rx_s.at[k], rx_r.at[k], pair).wait_recv()
            give(dx, dy)
    for dx in range(NX):
        for dy in range(NY):
            hand_on(1 - c, dx, dy).wait_recv()
    for cp in sends:
        cp.wait_send()


def body(hidden_acts, out_grads, momentum, weight_tiles, kept_ids, kept_counts):
    hbm = pl.BlockSpec(memory_space=pltpu.HBM)
    vmem = pl.BlockSpec(memory_space=pltpu.VMEM)

    def both(*shape):
        return [pltpu.VMEM(shape, BF16)] * 2

    def pairs(*counts):
        return [pltpu.SemaphoreType.DMA((n,)) for n in counts for _ in range(2)]

    dma = pltpu.SemaphoreType.DMA
    gathered, moment_out = pl.pallas_call(
        kernel,
        out_shape=(
            jax.ShapeDtypeStruct((NX, NY, 2, ROWS, 128), BF16),
            jax.ShapeDtypeStruct((ROWS, 128), F32),
        ),
        in_specs=[hbm] * 7,
        out_specs=(vmem, vmem),
        scratch_shapes=[
            pltpu.VMEM((256, 128), BF16),
            pltpu.VMEM((PARTS, 256, PART_COLS), BF16),
            pltpu.VMEM((ROWS, 128), F32),
            pltpu.VMEM((3, TILE_SQ), BF16),
            pltpu.SMEM((3, 1, 4), jnp.int32),
            pltpu.SMEM((1, 3), jnp.int32),
            pltpu.VMEM((448, 128), F32),
            pltpu.VMEM((2, NX, NY, ROWS, 128), BF16),
            pltpu.VMEM((NX, NY, ROWS, 128), BF16),
            pltpu.VMEM((ROWS, 128), F32),
            pltpu.VMEM((NZ, 16, 128), BF16),
            pltpu.VMEM((ROWS, 128), F32),
            pltpu.VMEM((NX, Y_ROWS, 128), F32),
            pltpu.VMEM((NY, ROWS - Y_ROWS, 128), F32),
            *both(NY - 1, NX, Y_ROWS, 128),
            *both(NX - 1, NY, ROWS - Y_ROWS, 128),
            *both(NY - 1, ROWS - Y_ROWS, 128),
            *both(NX - 1, Y_ROWS, 128),
            dma((PARTS,)),
            dma((6,)),
            *pairs(2 * PARTS, 7, 3, 7, 3, 7, 7, 3, 21, 21, 32),
        ],
        compiler_params=pltpu.CompilerParams(
            collective_id=0, has_side_effects=True, vmem_limit_bytes=56 * 1024 * 1024
        ),
    )(
        hidden_acts, out_grads, momentum.reshape(ROWS, 128), weight_tiles,
        kept_ids.transpose(1, 0, 2), kept_counts, jnp.asarray(constants()),
    )
    return gathered.reshape(192, TILE_SQ), moment_out.reshape(1, 3, TILE_SQ)


def solution(mesh):
    in_specs = (
        P("rep", "shard", None),
        P("rep", "shard", None),
        P("rep", "shard", None),
        P("shard", None),
        P("rep", "shard", None),
        P("rep", "shard"),
    )
    out_specs = (P(), P("rep", "shard", None))
    return jax.shard_map(body, mesh=mesh, in_specs=in_specs, out_specs=out_specs, check_vma=False)
```

```python
import math

import jax
import jax.numpy as jnp
import numpy as np
from jax import lax
from jax.experimental import pallas as pl
from jax.experimental.pallas import tpu as pltpu
from jax.sharding import PartitionSpec as P

TILE = 64
BLOCKS = 32
TILE_SQ = 4096
D = 6144
NX, NY, NZ = 4, 8, 8
ROWS = 96
Y_ROWS = 32
G_ROWS = 32
X_FAR = (2, 1, 3)
Y_FAR = (4, 3, 5, 2, 6, 1, 7)
X_PARTS = 2
PARTS = 4
PART_COLS = D // PARTS
PART_CHIPS = PART_COLS // 384
MOMENTUM_DECAY = 0.9
STEP = 2.0 / 8.0
GRAD_SCALE = 1.0 / 128.0
MESH = pl.DeviceIdType.MESH
F32 = jnp.float32
BF16 = jnp.bfloat16


def constants():
    k = np.arange(TILE, dtype=np.float64)[:, None]
    n = np.arange(TILE, dtype=np.float64)[None, :]
    basis = np.cos(math.pi * (2 * n + 1) * k / (2 * TILE))
    basis *= np.where(k == 0, math.sqrt(1 / TILE), math.sqrt(2 / TILE))
    even, odd = basis[:, 0::2], basis[:, 1::2]
    out = np.zeros((448, 128))
    out[0:128] = np.tile(basis.T, (2, 2))
    out[128:192, 0:64] = basis
    out[192:256, 64:128] = basis
    out[256:384, 0:32] = np.concatenate([even, odd], 0)
    out[384:448, 0:64] = np.concatenate([even.T, odd.T], 0)
    return out.astype(np.float32)


def dot32(a, b):
    return lax.dot_general(
        a, b, (((1,), (0,)), ((), ())), precision=lax.Precision.HIGHEST, preferred_element_type=F32
    )


def iota(shape, dim):
    return lax.broadcasted_iota(jnp.int32, shape, dim)


def kernel(
    hid, grads, mom, wts, ids, counts, consts,
    out, mom_out,
    gath, rows_f, hid_v, gbuf, mom_v, wts_v, ids_v, counts_v, consts_v,
    part, prx, wsum, zbuf, slab, acc_y, acc_x,
    st_y1, rx_y1, st_x1, rx_x1, st_y2, rx_y2, st_x2, rx_x2,
    load_sem, in_sem, pair_s, pair_r,
    y1_s, y1_r, x1_s, x1_r, y2_s, y2_r, x2_s, x2_r,
    z_s, z_r, gy_s, gy_r, gx_s, gx_r, ry_s, ry_r, rx_s, rx_r, fw_s, fw_r,
):
    shard, z = lax.axis_index("shard"), lax.axis_index("rep")
    c = shard % 2
    y = (shard // 2) % NY
    x = shard // (2 * NY)

    def dev(xx, yy, cc):
        return ((xx * NY + yy) * 2 + cc, z)

    def y_at(d):
        return (y + d) % NY

    def x_at(d):
        return (x + d) % NX

    def to_y(d):
        return dev(x, y_at(d), c)

    def to_x(d):
        return dev(x_at(d), y, c)

    def remote(src, dst, send, recv, who):
        return pltpu.make_async_remote_copy(
            src_ref=src, dst_ref=dst, send_sem=send, recv_sem=recv,
            device_id=who, device_id_type=MESH,
        )

    pair = dev(x, y, 1 - c)
    barrier = pltpu.get_barrier_semaphore()
    partners = [pair] + [to_x(d) for d in X_FAR] + [to_y(d) for d in Y_FAR]
    partners += [(shard, (z + d) % NZ) for d in range(1, NZ)]
    for who in partners:
        pl.semaphore_signal(barrier, inc=1, device_id=who, device_id_type=MESH)

    moves = []
    for k, (src, dst) in enumerate((
        (hid.at[0], hid_v), (mom, mom_v), (wts, wts_v), (ids, ids_v), (counts, counts_v),
        (consts, consts_v),
    )):
        moves.append(pltpu.make_async_copy(src, dst, in_sem.at[k]))
    moves[0].start()
    loads = []
    for p in range(PARTS):
        cp = pltpu.make_async_copy(
            grads.at[0, :, pl.ds(p * PART_COLS, PART_COLS)], gbuf.at[p], load_sem.at[p]
        )
        cp.start()
        loads.append(cp)
    for cp in moves[1:]:
        cp.start()
    moves[0].wait()

    r_, c_ = iota((128, 128), 0), iota((128, 128), 1)
    src = (r_ // 64) * 64 + (r_ % 32) * 2 + (r_ % 64) // 32
    perm = jnp.where(c_ == src, 1.0, 0.0).astype(BF16)
    hid_t = lax.dot_general(
        perm, hid_v[...], (((1,), (1,)), ((), ())), preferred_element_type=F32
    ).astype(BF16)

    left = iota((32, 128), 1) < 64
    for p in range(PARTS):
        loads[p].wait()
        full = jnp.dot(hid_t, gbuf[p], preferred_element_type=F32)
        for i in range(2):
            for q in range(PART_CHIPS):
                chip = i * 16 + p * PART_CHIPS + q
                for b in range(3):
                    cols = slice(q * 384 + b * 128, q * 384 + (b + 1) * 128)
                    ev = full[i * 64:i * 64 + 32, cols]
                    od = full[i * 64 + 32:i * 64 + 64, cols]
                    first = jnp.where(left, ev, pltpu.roll(od, 64, 1)).astype(BF16)
                    second = jnp.where(left, pltpu.roll(ev, 64, 1), od).astype(BF16)
                    for t, val in ((2 * b, first), (2 * b + 1, second)):
                        row = (t % 3) * 32
                        part[t // 3, chip // 8, chip % 8, row:row + 32, :] = val
    pl.semaphore_wait(barrier, len(partners))

    ys, xs = slice(0, Y_ROWS), slice(Y_ROWS, ROWS)
    every = slice(None)
    y_rows, x_rows = pl.ds(0, Y_ROWS), pl.ds(Y_ROWS, ROWS - Y_ROWS)
    pair_copies = []
    for k, ix in enumerate(
        [(x_at(d), every, x_rows) for d in X_FAR] + [(every, every, y_rows), (x, every, x_rows)]
    ):
        cp = remote(part.at[(1 - c,) + ix], prx.at[ix], pair_s.at[k], pair_r.at[k], pair)
        cp.start()
        pair_copies.append(cp)

    def own(ix):
        return part[(c,) + ix].astype(F32) + prx[ix].astype(F32)

    first_x, first_y, second_y, second_x = [], [], [], []
    order = Y_FAR + (0,)
    step = NY // X_PARTS
    for part_no in range(X_PARTS):
        ks = range(part_no * step, (part_no + 1) * step)
        for i, d in enumerate(X_FAR):
            if part_no == 0:
                pair_copies[i].wait_recv()
            for k in ks:
                st_x1[d - 1, k] = own((x_at(d), y_at(order[k]), xs)).astype(BF16)
            at = pl.ds(part_no * step, step)
            n = (d - 1) * X_PARTS + part_no
            cp = remote(st_x1.at[d - 1, at], rx_x1.at[d - 1, at], x1_s.at[n], x1_r.at[n], to_x(d))
            cp.start()
            first_x.append(cp)
        if part_no == 0:
            pair_copies[3].wait_recv()
            for d in Y_FAR:
                st_y1[d - 1] = own((every, y_at(d), ys)).astype(BF16)
                cp = remote(st_y1.at[d - 1], rx_y1.at[d - 1], y1_s.at[d - 1], y1_r.at[d - 1], to_y(d))
                cp.start()
                first_y.append(cp)
    pair_copies[4].wait_recv()
    for part_no in range(X_PARTS):
        for cp in first_x[3 * part_no:3 * part_no + 3]:
            cp.wait_recv()
        for k in range(part_no * step, (part_no + 1) * step):
            total = own((x, y_at(order[k]), xs))
            for d in X_FAR:
                total = total + rx_x1[d - 1, k].astype(F32)
            d = order[k]
            if d == 0:
                acc_x[...] = total
                continue
            st_y2[d - 1] = total.astype(BF16)
            cp = remote(st_y2.at[d - 1], rx_y2.at[d - 1], y2_s.at[d - 1], y2_r.at[d - 1], to_y(d))
            cp.start()
            second_y.append(cp)
    total = own((every, y, ys))
    for cp, d in zip(first_y, Y_FAR):
        cp.wait_recv()
        total = total + rx_y1[d - 1].astype(F32)
    acc_y[...] = total
    for d in X_FAR:
        st_x2[d - 1] = acc_y[x_at(d)].astype(BF16)
        cp = remote(st_x2.at[d - 1], rx_x2.at[d - 1], x2_s.at[d - 1], x2_r.at[d - 1], to_x(d))
        cp.start()
        second_x.append(cp)
    total = acc_x[...]
    for cp, d in zip(second_y, Y_FAR):
        cp.wait_recv()
        total = total + rx_y2[d - 1].astype(F32)
    slab[xs] = total
    total = acc_y[x]
    for cp, d in zip(second_x, X_FAR):
        cp.wait_recv()
        total = total + rx_x2[d - 1].astype(F32)
    slab[ys] = total
    for cp in moves[1:]:
        cp.wait()

    moment = MOMENTUM_DECAY * mom_v[...] + GRAD_SCALE * slab[...]
    both, diag = consts_v[0:128], consts_v[128:256]
    fwd, inv = consts_v[256:384, 0:32], consts_v[384:448, 0:64]
    tiles = jnp.concatenate([moment[0:32], moment[32:64], moment[64:96]], axis=1)
    v = dot32(fwd, tiles)
    left64 = iota((64, 128), 1) < 64
    v = jnp.concatenate(
        [
            jnp.where(left64, v[0:64, k * 128:(k + 1) * 128], v[64:128, k * 128:(k + 1) * 128])
            for k in range(3)
        ],
        axis=0,
    )
    coef = dot32(v, both)

    group = (iota((64, 128), 1) % 64) // 16
    unit = (iota((64, 128), 0) // 8) * 4 + group
    kept = []
    for k in range(3):
        keep = jnp.zeros((64, 128), F32)
        for j in range(4):
            live = jnp.where(j < counts_v[0, k], ids_v[k, 0, j], -1)
            keep = jnp.where(unit == live, 1.0, keep)
        kept.append(coef[k * 64:(k + 1) * 64] * keep)

    lane8 = iota((8, 128), 1)
    row8 = iota((8, 128), 0)
    picked = []
    numbers = jnp.zeros((8, 128), F32)
    for k in range(3):
        for j in range(4):
            number = ids_v[k, 0, j]
            block = jnp.zeros((8, 128), F32)
            for p in range(8):
                block = jnp.where(number // 4 == p, kept[k][p * 8:(p + 1) * 8], block)
            here = (lane8 // 16) == number % 4
            picked.append(jnp.where(here & (j < counts_v[0, k]), block, 0.0))
            slot = (row8 == k) & (lane8 // 16 == 4 + j)
            numbers = jnp.where(slot, number.astype(F32), numbers)
    picked = jnp.concatenate(picked, axis=0).astype(BF16)
    spread = jnp.where(
        iota((128, 128), 0) % 16 == iota((128, 128), 1) % 16, 1.0, 0.0
    ).astype(BF16)
    picked = jnp.dot(picked, spread, preferred_element_type=F32)
    halves = [jnp.zeros((8, 128), F32), numbers]
    for k in range(3):
        for j in range(4):
            at = (k * 4 + j) * 8
            halves[k // 2] = jnp.where(
                lane8 // 16 == (k % 2) * 4 + j, picked[at:at + 8], halves[k // 2]
            )
    zbuf[z] = jnp.concatenate(halves, axis=0).astype(BF16)
    sends = []
    for d in range(1, NZ):
        cp = pltpu.make_async_remote_copy(
            src_ref=zbuf.at[z], dst_ref=zbuf.at[z],
            send_sem=z_s.at[d - 1], recv_sem=z_r.at[d - 1],
            device_id=(shard, (z + d) % NZ), device_id_type=MESH,
        )
        cp.start()
        sends.append(cp)

    def inverse(rows):
        kb = dot32(rows, diag)
        kb = jnp.concatenate([kb[0:64], kb[64:128], kb[128:192]], axis=1)
        w = dot32(inv, kb)
        return jnp.concatenate(
            [
                jnp.where(left, w[0:32, k * 128:(k + 1) * 128], w[32:64, k * 128:(k + 1) * 128])
                for k in range(3)
            ],
            axis=0,
        )

    mom_out[...] = moment - inverse(jnp.concatenate(kept, axis=0))
    for m in range(32):
        wsum[pl.ds(m, 3, stride=32), :] = wts_v[:, m * 128:(m + 1) * 128].astype(F32)

    for d in range(1, NZ):
        frm = (z + NZ - d) % NZ
        pltpu.make_async_remote_copy(
            src_ref=zbuf.at[z], dst_ref=zbuf.at[frm],
            send_sem=z_s.at[d - 1], recv_sem=z_r.at[d - 1],
            device_id=(shard, frm), device_id_type=MESH,
        ).wait_recv()

    wide = iota((128, 1024), 1)
    pick = (wide // 128 == iota((128, 1024), 0) // 16) & (wide % 16 == iota((128, 1024), 0) % 16)
    pick = jnp.where(pick, 1.0, 0.0).astype(BF16)
    msgs = jnp.concatenate([zbuf[r] for r in range(NZ)], axis=0)
    vals = jnp.dot(msgs, pick, preferred_element_type=F32)
    unitf = unit.astype(F32)
    totals = []
    for k in range(3):
        total = jnp.zeros((64, 128), F32)
        for r in range(NZ):
            for j in range(4):
                col = ((k % 2) * 4 + j) * 128
                row = r * 16 + (k // 2) * 8
                val = vals[row:row + 8, col:col + 128]
                num = vals[r * 16 + 8 + k:r * 16 + 9 + k, (4 + j) * 128:(5 + j) * 128]
                val = jnp.concatenate([val] * 8, axis=0)
                total = total + jnp.where(unitf == num, val, 0.0)
        totals.append(total)
    update = inverse(jnp.concatenate(totals, axis=0))
    gath[x, y, c] = (wsum[...] - STEP * update).astype(BF16)


    sends += pair_copies + first_x + first_y + second_x + second_y
    lower, upper = pl.ds(0, G_ROWS), pl.ds(G_ROWS, ROWS - G_ROWS)

    def same(ref, send, recv, who):
        return remote(ref, ref, send, recv, who)

    mine = gath.at[x, y, c]
    for d in X_FAR:
        cp = same(mine, gx_s.at[d - 1], gx_r.at[d - 1], to_x(d))
        cp.start()
        sends.append(cp)
    for d in Y_FAR:
        cp = same(mine, gy_s.at[d - 1], gy_r.at[d - 1], to_y(d))
        cp.start()
        sends.append(cp)

    def hand_on(cc, dx, dy):
        k = dx * NY + dy
        return same(gath.at[x_at(NX - dx), y_at(NY - dy), cc], fw_s.at[k], fw_r.at[k], pair)

    def place(cc, dx, dy):
        xx, yy = x_at(NX - dx), y_at(NY - dy)
        tile = ((xx * NY + yy) * 2 + cc) * 3
        val = gath[xx, yy, cc].astype(F32)
        for k in range(3):
            rows_f[pl.ds(tile + k, 32, stride=192), :] = val[k * 32:(k + 1) * 32]

    def give(dx, dy):
        cp = hand_on(c, dx, dy)
        cp.start()
        sends.append(cp)

    give(0, 0)
    place(c, 0, 0)
    for dx in X_FAR:
        src = gath.at[x_at(NX - dx), y, c]
        same(src, gx_s.at[dx - 1], gx_r.at[dx - 1], pair).wait_recv()
        for dy in Y_FAR:
            k = (dx - 1) * 7 + dy - 1
            cp = same(src.at[lower], ry_s.at[k], ry_r.at[k], to_y(dy))
            cp.start()
            sends.append(cp)
        give(dx, 0)
        place(c, dx, 0)
    for dy in Y_FAR:
        src = gath.at[x, y_at(NY - dy), c]
        same(src, gy_s.at[dy - 1], gy_r.at[dy - 1], pair).wait_recv()
        for dx in X_FAR:
            k = (dx - 1) * 7 + dy - 1
            cp = same(src.at[upper], rx_s.at[k], rx_r.at[k], to_x(dx))
            cp.start()
            sends.append(cp)
        give(0, dy)
        place(c, 0, dy)
    for dy in Y_FAR:
        for dx in X_FAR:
            k = (dx - 1) * 7 + dy - 1
            dst = gath.at[x_at(NX - dx), y_at(NY - dy), c]
            same(dst.at[lower], ry_s.at[k], ry_r.at[k], pair).wait_recv()
            same(dst.at[upper], rx_s.at[k], rx_r.at[k], pair).wait_recv()
            give(dx, dy)
            place(c, dx, dy)
    for dx, dy in (
        [(0, 0)] + [(d, 0) for d in X_FAR] + [(0, d) for d in Y_FAR]
        + [(dx, dy) for dy in Y_FAR for dx in X_FAR]
    ):
        hand_on(1 - c, dx, dy).wait_recv()
        place(1 - c, dx, dy)
    for m in range(32):
        out[:, m * 128:(m + 1) * 128] = rows_f[m * 192:(m + 1) * 192].astype(BF16)
    for cp in sends:
        cp.wait_send()


def body(hidden_acts, out_grads, momentum, weight_tiles, kept_ids, kept_counts):
    hbm = pl.BlockSpec(memory_space=pltpu.HBM)
    vmem = pl.BlockSpec(memory_space=pltpu.VMEM)

    def both(*shape):
        return [pltpu.VMEM(shape, BF16)] * 2

    def pairs(*counts):
        return [pltpu.SemaphoreType.DMA((n,)) for n in counts for _ in range(2)]

    dma = pltpu.SemaphoreType.DMA
    gathered, moment_out = pl.pallas_call(
        kernel,
        out_shape=(
            jax.ShapeDtypeStruct((192, TILE_SQ), BF16),
            jax.ShapeDtypeStruct((ROWS, 128), F32),
        ),
        in_specs=[hbm] * 7,
        out_specs=(vmem, vmem),
        scratch_shapes=[
            pltpu.VMEM((NX, NY, 2, ROWS, 128), BF16),
            pltpu.VMEM((32 * 192, 128), F32),
            pltpu.VMEM((256, 128), BF16),
            pltpu.VMEM((PARTS, 256, PART_COLS), BF16),
            pltpu.VMEM((ROWS, 128), F32),
            pltpu.VMEM((3, TILE_SQ), BF16),
            pltpu.SMEM((3, 1, 4), jnp.int32),
            pltpu.SMEM((1, 3), jnp.int32),
            pltpu.VMEM((448, 128), F32),
            pltpu.VMEM((2, NX, NY, ROWS, 128), BF16),
            pltpu.VMEM((NX, NY, ROWS, 128), BF16),
            pltpu.VMEM((ROWS, 128), F32),
            pltpu.VMEM((NZ, 16, 128), BF16),
            pltpu.VMEM((ROWS, 128), F32),
            pltpu.VMEM((NX, Y_ROWS, 128), F32),
            pltpu.VMEM((ROWS - Y_ROWS, 128), F32),
            *both(NY - 1, NX, Y_ROWS, 128),
            *both(NX - 1, NY, ROWS - Y_ROWS, 128),
            *both(NY - 1, ROWS - Y_ROWS, 128),
            *both(NX - 1, Y_ROWS, 128),
            dma((PARTS,)),
            dma((6,)),
            *pairs(5, 7, 3 * X_PARTS, 7, 3, 7, 7, 3, 21, 21, 32),
        ],
        compiler_params=pltpu.CompilerParams(
            collective_id=0, has_side_effects=True, vmem_limit_bytes=48 * 1024 * 1024
        ),
    )(*(
        pltpu.with_memory_space_constraint(arg, pltpu.HBM)
        for arg in (
            hidden_acts, out_grads, momentum.reshape(ROWS, 128), weight_tiles,
            kept_ids.transpose(1, 0, 2), kept_counts, jnp.asarray(constants()),
        )
    ))
    return gathered, moment_out.reshape(1, 3, TILE_SQ)


def solution(mesh):
    in_specs = (
        P("rep", "shard", None),
        P("rep", "shard", None),
        P("rep", "shard", None),
        P("shard", None),
        P("rep", "shard", None),
        P("rep", "shard"),
    )
    out_specs = (P(), P("rep", "shard", None))
    return jax.shard_map(body, mesh=mesh, in_specs=in_specs, out_specs=out_specs, check_vma=False)
```

```python
import math

import jax
import jax.numpy as jnp
import numpy as np
from jax import lax
from jax.experimental import pallas as pl
from jax.experimental.pallas import tpu as pltpu
from jax.sharding import PartitionSpec as P

TILE = 64
BLOCKS = 32
TILE_SQ = 4096
D = 6144
NX, NY, NZ = 4, 8, 8
ROWS = 96
Y_ROWS = 32
G_ROWS = 32
X_FAR = (2, 1, 3)
Y_FAR = (4, 3, 5, 2, 6, 1, 7)
OFFSETS = (0,) + Y_FAR
K_GROUPS = ((1, 3), (3, 5), (5, 8))
X_PARTS = 2
PARTS = 4
PART_COLS = D // PARTS
PART_CHIPS = PART_COLS // 384
MOMENTUM_DECAY = 0.9
STEP = 2.0 / 8.0
GRAD_SCALE = 1.0 / 128.0
MESH = pl.DeviceIdType.MESH
F32 = jnp.float32
BF16 = jnp.bfloat16


def constants():
    k = np.arange(TILE, dtype=np.float64)[:, None]
    n = np.arange(TILE, dtype=np.float64)[None, :]
    basis = np.cos(math.pi * (2 * n + 1) * k / (2 * TILE))
    basis *= np.where(k == 0, math.sqrt(1 / TILE), math.sqrt(2 / TILE))
    even, odd = basis[:, 0::2], basis[:, 1::2]
    out = np.zeros((448, 128))
    out[0:128] = np.tile(basis.T, (2, 2))
    out[128:192, 0:64] = basis
    out[192:256, 64:128] = basis
    out[256:384, 0:32] = np.concatenate([even, odd], 0)
    out[384:448, 0:64] = np.concatenate([even.T, odd.T], 0)
    return out.astype(np.float32)


def dot32(a, b):
    return lax.dot_general(
        a, b, (((1,), (0,)), ((), ())), precision=lax.Precision.HIGHEST, preferred_element_type=F32
    )


def iota(shape, dim):
    return lax.broadcasted_iota(jnp.int32, shape, dim)


def kernel(
    hid, grads, mom, wts, ids, counts, consts,
    out, mom_out,
    gath, rows_f, hid_v, gbuf, mom_v, wts_v, ids_v, counts_v, consts_v,
    part, prx, wsum, zbuf, slab, acc_y, acc_x,
    st_y1, rx_y1, st_x1, rx_x1, st_y2, rx_y2, st_x2, rx_x2,
    load_sem, in_sem, pair_s, pair_r,
    y1_s, y1_r, x1_s, x1_r, y2_s, y2_r, x2_s, x2_r,
    z_s, z_r, gy_s, gy_r, gx_s, gx_r, ry_s, ry_r, rx_s, rx_r, fw_s, fw_r,
):
    shard, z = lax.axis_index("shard"), lax.axis_index("rep")
    c = shard % 2
    y = (shard // 2) % NY
    x = shard // (2 * NY)

    def dev(xx, yy, cc):
        return ((xx * NY + yy) * 2 + cc, z)

    def y_at(d):
        return (y + d) % NY

    def x_at(d):
        return (x + d) % NX

    def to_y(d):
        return dev(x, y_at(d), c)

    def to_x(d):
        return dev(x_at(d), y, c)

    def remote(src, dst, send, recv, who):
        return pltpu.make_async_remote_copy(
            src_ref=src, dst_ref=dst, send_sem=send, recv_sem=recv,
            device_id=who, device_id_type=MESH,
        )

    pair = dev(x, y, 1 - c)
    barrier = pltpu.get_barrier_semaphore()
    partners = [pair] + [to_x(d) for d in X_FAR] + [to_y(d) for d in Y_FAR]
    partners += [(shard, (z + d) % NZ) for d in range(1, NZ)]
    for who in partners:
        pl.semaphore_signal(barrier, inc=1, device_id=who, device_id_type=MESH)

    moves = []
    for k, (src, dst) in enumerate((
        (hid.at[0], hid_v), (mom, mom_v), (wts, wts_v), (ids, ids_v), (counts, counts_v),
        (consts, consts_v),
    )):
        moves.append(pltpu.make_async_copy(src, dst, in_sem.at[k]))
    moves[0].start()
    loads = []
    for p in range(PARTS):
        cp = pltpu.make_async_copy(
            grads.at[0, :, pl.ds(p * PART_COLS, PART_COLS)], gbuf.at[p], load_sem.at[p]
        )
        cp.start()
        loads.append(cp)
    for cp in moves[1:]:
        cp.start()
    moves[0].wait()

    r_, c_ = iota((128, 128), 0), iota((128, 128), 1)
    src = (r_ // 64) * 64 + (r_ % 32) * 2 + (r_ % 64) // 32
    perm = jnp.where(c_ == src, 1.0, 0.0).astype(BF16)
    hid_t = lax.dot_general(
        perm, hid_v[...], (((1,), (1,)), ((), ())), preferred_element_type=F32
    ).astype(BF16)

    left = iota((32, 128), 1) < 64
    for p in range(PARTS):
        loads[p].wait()
        full = jnp.dot(hid_t, gbuf[p], preferred_element_type=F32)
        for i in range(2):
            for q in range(PART_CHIPS):
                chip = i * 16 + p * PART_CHIPS + q
                for b in range(3):
                    cols = slice(q * 384 + b * 128, q * 384 + (b + 1) * 128)
                    ev = full[i * 64:i * 64 + 32, cols]
                    od = full[i * 64 + 32:i * 64 + 64, cols]
                    first = jnp.where(left, ev, pltpu.roll(od, 64, 1)).astype(BF16)
                    second = jnp.where(left, pltpu.roll(ev, 64, 1), od).astype(BF16)
                    for t, val in ((2 * b, first), (2 * b + 1, second)):
                        row = (t % 3) * 32
                        part[t // 3, chip // 8, chip % 8, row:row + 32, :] = val
    pl.semaphore_wait(barrier, len(partners))

    ys, xs = slice(0, Y_ROWS), slice(Y_ROWS, ROWS)
    every = slice(None)
    y_rows, x_rows = pl.ds(0, Y_ROWS), pl.ds(Y_ROWS, ROWS - Y_ROWS)
    pair_copies = []
    for k, ix in enumerate(
        [(x_at(d), every, x_rows) for d in X_FAR] + [(every, every, y_rows), (x, every, x_rows)]
    ):
        cp = remote(part.at[(1 - c,) + ix], prx.at[ix], pair_s.at[k], pair_r.at[k], pair)
        cp.start()
        pair_copies.append(cp)

    def own(ix):
        return part[(c,) + ix] + prx[ix]

    first_x, first_y, second_y, second_x = [], [], [], []
    order = Y_FAR + (0,)
    step = NY // X_PARTS
    for part_no in range(X_PARTS):
        ks = range(part_no * step, (part_no + 1) * step)
        for i, d in enumerate(X_FAR):
            if part_no == 0:
                pair_copies[i].wait_recv()
            for k in ks:
                st_x1[d - 1, k] = own((x_at(d), y_at(order[k]), xs))
            at = pl.ds(part_no * step, step)
            n = (d - 1) * X_PARTS + part_no
            cp = remote(st_x1.at[d - 1, at], rx_x1.at[d - 1, at], x1_s.at[n], x1_r.at[n], to_x(d))
            cp.start()
            first_x.append(cp)
        if part_no == 0:
            pair_copies[3].wait_recv()
            for d in Y_FAR:
                st_y1[d - 1] = own((every, y_at(d), ys))
                cp = remote(st_y1.at[d - 1], rx_y1.at[d - 1], y1_s.at[d - 1], y1_r.at[d - 1], to_y(d))
                cp.start()
                first_y.append(cp)
    pair_copies[4].wait_recv()
    for part_no in range(X_PARTS):
        for cp in first_x[3 * part_no:3 * part_no + 3]:
            cp.wait_recv()
        for k in range(part_no * step, (part_no + 1) * step):
            total = own((x, y_at(order[k]), xs)).astype(F32)
            for d in X_FAR:
                total = total + rx_x1[d - 1, k].astype(F32)
            d = order[k]
            if d == 0:
                acc_x[...] = total
                continue
            st_y2[d - 1] = total.astype(BF16)
            cp = remote(st_y2.at[d - 1], rx_y2.at[d - 1], y2_s.at[d - 1], y2_r.at[d - 1], to_y(d))
            cp.start()
            second_y.append(cp)
    total = own((every, y, ys)).astype(F32)
    for cp, d in zip(first_y, Y_FAR):
        cp.wait_recv()
        total = total + rx_y1[d - 1].astype(F32)
    acc_y[...] = total
    for d in X_FAR:
        st_x2[d - 1] = acc_y[x_at(d)].astype(BF16)
        cp = remote(st_x2.at[d - 1], rx_x2.at[d - 1], x2_s.at[d - 1], x2_r.at[d - 1], to_x(d))
        cp.start()
        second_x.append(cp)
    total = acc_x[...]
    for cp, d in zip(second_y, Y_FAR):
        cp.wait_recv()
        total = total + rx_y2[d - 1].astype(F32)
    slab[xs] = total
    total = acc_y[x]
    for cp, d in zip(second_x, X_FAR):
        cp.wait_recv()
        total = total + rx_x2[d - 1].astype(F32)
    slab[ys] = total
    for cp in moves[1:]:
        cp.wait()

    moment = MOMENTUM_DECAY * mom_v[...] + GRAD_SCALE * slab[...]
    both, diag = consts_v[0:128], consts_v[128:256]
    fwd, inv = consts_v[256:384, 0:32], consts_v[384:448, 0:64]
    tiles = jnp.concatenate([moment[0:32], moment[32:64], moment[64:96]], axis=1)
    v = dot32(fwd, tiles)
    left64 = iota((64, 128), 1) < 64
    v = jnp.concatenate(
        [
            jnp.where(left64, v[0:64, k * 128:(k + 1) * 128], v[64:128, k * 128:(k + 1) * 128])
            for k in range(3)
        ],
        axis=0,
    )
    coef = dot32(v, both)

    group = (iota((64, 128), 1) % 64) // 16
    unit = (iota((64, 128), 0) // 8) * 4 + group
    kept = []
    for k in range(3):
        keep = jnp.zeros((64, 128), F32)
        for j in range(4):
            live = jnp.where(j < counts_v[0, k], ids_v[k, 0, j], -1)
            keep = jnp.where(unit == live, 1.0, keep)
        kept.append(coef[k * 64:(k + 1) * 64] * keep)

    lane8 = iota((8, 128), 1)
    row8 = iota((8, 128), 0)
    picked = []
    numbers = jnp.zeros((8, 128), F32)
    for k in range(3):
        for j in range(4):
            number = ids_v[k, 0, j]
            block = jnp.zeros((8, 128), F32)
            for p in range(8):
                block = jnp.where(number // 4 == p, kept[k][p * 8:(p + 1) * 8], block)
            here = (lane8 // 16) == number % 4
            picked.append(jnp.where(here & (j < counts_v[0, k]), block, 0.0))
            slot = (row8 == k) & (lane8 // 16 == 4 + j)
            numbers = jnp.where(slot, number.astype(F32), numbers)
    picked = jnp.concatenate(picked, axis=0).astype(BF16)
    spread = jnp.where(
        iota((128, 128), 0) % 16 == iota((128, 128), 1) % 16, 1.0, 0.0
    ).astype(BF16)
    picked = jnp.dot(picked, spread, preferred_element_type=F32)
    halves = [jnp.zeros((8, 128), F32), numbers]
    for k in range(3):
        for j in range(4):
            at = (k * 4 + j) * 8
            halves[k // 2] = jnp.where(
                lane8 // 16 == (k % 2) * 4 + j, picked[at:at + 8], halves[k // 2]
            )
    zbuf[z] = jnp.concatenate(halves, axis=0).astype(BF16)
    sends = []
    for d in range(1, NZ):
        cp = pltpu.make_async_remote_copy(
            src_ref=zbuf.at[z], dst_ref=zbuf.at[z],
            send_sem=z_s.at[d - 1], recv_sem=z_r.at[d - 1],
            device_id=(shard, (z + d) % NZ), device_id_type=MESH,
        )
        cp.start()
        sends.append(cp)

    def inverse(rows):
        kb = dot32(rows, diag)
        kb = jnp.concatenate([kb[0:64], kb[64:128], kb[128:192]], axis=1)
        w = dot32(inv, kb)
        return jnp.concatenate(
            [
                jnp.where(left, w[0:32, k * 128:(k + 1) * 128], w[32:64, k * 128:(k + 1) * 128])
                for k in range(3)
            ],
            axis=0,
        )

    mom_out[...] = moment - inverse(jnp.concatenate(kept, axis=0))
    for m in range(32):
        wsum[pl.ds(m, 3, stride=32), :] = wts_v[:, m * 128:(m + 1) * 128].astype(F32)

    for d in range(1, NZ):
        frm = (z + NZ - d) % NZ
        pltpu.make_async_remote_copy(
            src_ref=zbuf.at[z], dst_ref=zbuf.at[frm],
            send_sem=z_s.at[d - 1], recv_sem=z_r.at[d - 1],
            device_id=(shard, frm), device_id_type=MESH,
        ).wait_recv()

    wide = iota((128, 1024), 1)
    pick = (wide // 128 == iota((128, 1024), 0) // 16) & (wide % 16 == iota((128, 1024), 0) % 16)
    pick = jnp.where(pick, 1.0, 0.0).astype(BF16)
    msgs = jnp.concatenate([zbuf[r] for r in range(NZ)], axis=0)
    vals = jnp.dot(msgs, pick, preferred_element_type=F32)
    unitf = unit.astype(F32)
    totals = []
    for k in range(3):
        total = jnp.zeros((64, 128), F32)
        for r in range(NZ):
            for j in range(4):
                col = ((k % 2) * 4 + j) * 128
                row = r * 16 + (k // 2) * 8
                val = vals[row:row + 8, col:col + 128]
                num = vals[r * 16 + 8 + k:r * 16 + 9 + k, (4 + j) * 128:(5 + j) * 128]
                val = jnp.concatenate([val] * 8, axis=0)
                total = total + jnp.where(unitf == num, val, 0.0)
        totals.append(total)
    update = inverse(jnp.concatenate(totals, axis=0))
    gath[x, 0, c] = (wsum[...] - STEP * update).astype(BF16)


    sends += pair_copies + first_x + first_y + second_x + second_y
    lower, upper = pl.ds(0, G_ROWS), pl.ds(G_ROWS, ROWS - G_ROWS)

    def go(src, dst, send, recv, who):
        cp = remote(src, dst, send, recv, who)
        cp.start()
        sends.append(cp)

    def got(dst, send, recv):
        remote(dst, dst, send, recv, pair).wait_recv()

    def place(cc, i, k):
        tile = ((i * NY + y_at(NY - OFFSETS[k])) * 2 + cc) * 3
        val = gath[i, k, cc].astype(F32)
        for t in range(3):
            rows_f[pl.ds(tile + t, 32, stride=192), :] = val[t * 32:(t + 1) * 32]

    def slabs(cc, lo, hi):
        return gath.at[:, pl.ds(lo, hi - lo), cc]

    for d in X_FAR:
        mine = gath.at[x, 0, c]
        go(mine, mine, gx_s.at[d - 1], gx_r.at[d - 1], to_x(d))
    for k in range(1, NY):
        go(
            gath.at[x, 0, c, upper], gath.at[x, k, c, upper], gy_s.at[k - 1], gy_r.at[k - 1],
            to_y(OFFSETS[k]),
        )
    for d in X_FAR:
        got(gath.at[x_at(NX - d), 0, c], gx_s.at[d - 1], gx_r.at[d - 1])
    for k in range(1, NY):
        go(
            gath.at[:, 0, c, lower], gath.at[:, k, c, lower], ry_s.at[k - 1], ry_r.at[k - 1],
            to_y(OFFSETS[k]),
        )
    go(slabs(c, 0, 1), slabs(c, 0, 1), fw_s.at[0], fw_r.at[0], pair)
    for i in range(NX):
        place(c, i, 0)
    for n, (lo, hi) in enumerate(K_GROUPS):
        for k in range(lo, hi):
            got(gath.at[x, k, c, upper], gy_s.at[k - 1], gy_r.at[k - 1])
        for d in X_FAR:
            ref = gath.at[x, pl.ds(lo, hi - lo), c, upper]
            m = n * 3 + d - 1
            go(ref, ref, rx_s.at[m], rx_r.at[m], to_x(d))
    got(slabs(1 - c, 0, 1), fw_s.at[0], fw_r.at[0])
    for i in range(NX):
        place(1 - c, i, 0)
    for n, (lo, hi) in enumerate(K_GROUPS):
        for k in range(lo, hi):
            got(gath.at[:, k, c, lower], ry_s.at[k - 1], ry_r.at[k - 1])
        for d in X_FAR:
            m = n * 3 + d - 1
            got(gath.at[x_at(NX - d), pl.ds(lo, hi - lo), c, upper], rx_s.at[m], rx_r.at[m])
        go(slabs(c, lo, hi), slabs(c, lo, hi), fw_s.at[n + 1], fw_r.at[n + 1], pair)
        for k in range(lo, hi):
            for i in range(NX):
                place(c, i, k)
    for n, (lo, hi) in enumerate(K_GROUPS):
        got(slabs(1 - c, lo, hi), fw_s.at[n + 1], fw_r.at[n + 1])
        for k in range(lo, hi):
            for i in range(NX):
                place(1 - c, i, k)
    for m in range(32):
        out[:, m * 128:(m + 1) * 128] = rows_f[m * 192:(m + 1) * 192].astype(BF16)
    for cp in sends:
        cp.wait_send()


def body(hidden_acts, out_grads, momentum, weight_tiles, kept_ids, kept_counts):
    hbm = pl.BlockSpec(memory_space=pltpu.HBM)
    vmem = pl.BlockSpec(memory_space=pltpu.VMEM)

    def both(*shape):
        return [pltpu.VMEM(shape, BF16)] * 2

    def pairs(*counts):
        return [pltpu.SemaphoreType.DMA((n,)) for n in counts for _ in range(2)]

    dma = pltpu.SemaphoreType.DMA
    gathered, moment_out = pl.pallas_call(
        kernel,
        out_shape=(
            jax.ShapeDtypeStruct((192, TILE_SQ), BF16),
            jax.ShapeDtypeStruct((ROWS, 128), F32),
        ),
        in_specs=[hbm] * 7,
        out_specs=(vmem, vmem),
        scratch_shapes=[
            pltpu.VMEM((NX, NY, 2, ROWS, 128), BF16),
            pltpu.VMEM((32 * 192, 128), F32),
            pltpu.VMEM((256, 128), BF16),
            pltpu.VMEM((PARTS, 256, PART_COLS), BF16),
            pltpu.VMEM((ROWS, 128), F32),
            pltpu.VMEM((3, TILE_SQ), BF16),
            pltpu.SMEM((3, 1, 4), jnp.int32),
            pltpu.SMEM((1, 3), jnp.int32),
            pltpu.VMEM((448, 128), F32),
            pltpu.VMEM((2, NX, NY, ROWS, 128), BF16),
            pltpu.VMEM((NX, NY, ROWS, 128), BF16),
            pltpu.VMEM((ROWS, 128), F32),
            pltpu.VMEM((NZ, 16, 128), BF16),
            pltpu.VMEM((ROWS, 128), F32),
            pltpu.VMEM((NX, Y_ROWS, 128), F32),
            pltpu.VMEM((ROWS - Y_ROWS, 128), F32),
            *both(NY - 1, NX, Y_ROWS, 128),
            *both(NX - 1, NY, ROWS - Y_ROWS, 128),
            *both(NY - 1, ROWS - Y_ROWS, 128),
            *both(NX - 1, Y_ROWS, 128),
            dma((PARTS,)),
            dma((6,)),
            *pairs(5, 7, 3 * X_PARTS, 7, 3, 7, 7, 3, 7, 3 * len(K_GROUPS), 1 + len(K_GROUPS)),
        ],
        compiler_params=pltpu.CompilerParams(
            collective_id=0, has_side_effects=True, vmem_limit_bytes=48 * 1024 * 1024
        ),
    )(*(
        pltpu.with_memory_space_constraint(arg, pltpu.HBM)
        for arg in (
            hidden_acts, out_grads, momentum.reshape(ROWS, 128), weight_tiles,
            kept_ids.transpose(1, 0, 2), kept_counts, jnp.asarray(constants()),
        )
    ))
    return gathered, moment_out.reshape(1, 3, TILE_SQ)


def solution(mesh):
    in_specs = (
        P("rep", "shard", None),
        P("rep", "shard", None),
        P("rep", "shard", None),
        P("shard", None),
        P("rep", "shard", None),
        P("rep", "shard"),
    )
    out_specs = (P(), P("rep", "shard", None))
    return jax.shard_map(body, mesh=mesh, in_specs=in_specs, out_specs=out_specs, check_vma=False)
```

```python
import math

import jax
import jax.numpy as jnp
import numpy as np
from jax import lax
from jax.experimental import pallas as pl
from jax.experimental.pallas import tpu as pltpu
from jax.sharding import PartitionSpec as P

TILE = 64
BLOCKS = 32
TILE_SQ = 4096
D = 6144
NX, NY, NZ = 4, 8, 8
ROWS = 96
Y_ROWS = 32
G_ROWS = 32
X_FAR = (2, 1, 3)
Y_FAR = (4, 3, 5, 2, 6, 1, 7)
OFFSETS = (0,) + Y_FAR
K_GROUPS = ((1, 3), (3, 5), (5, 8))
X_PARTS = 2
PARTS = 4
PART_COLS = D // PARTS
PART_CHIPS = PART_COLS // 384
MOMENTUM_DECAY = 0.9
STEP = 2.0 / 8.0
GRAD_SCALE = 1.0 / 128.0
MESH = pl.DeviceIdType.MESH
F32 = jnp.float32
BF16 = jnp.bfloat16


def constants():
    k = np.arange(TILE, dtype=np.float64)[:, None]
    n = np.arange(TILE, dtype=np.float64)[None, :]
    basis = np.cos(math.pi * (2 * n + 1) * k / (2 * TILE))
    basis *= np.where(k == 0, math.sqrt(1 / TILE), math.sqrt(2 / TILE))
    even, odd = basis[:, 0::2], basis[:, 1::2]
    out = np.zeros((448, 128))
    out[0:128] = np.tile(basis.T, (2, 2))
    out[128:192, 0:64] = basis
    out[192:256, 64:128] = basis
    out[256:384, 0:32] = np.concatenate([even, odd], 0)
    out[384:448, 0:64] = np.concatenate([even.T, odd.T], 0)
    return out.astype(np.float32)


def dot32(a, b):
    def dot(u, v):
        return jnp.dot(u, v, preferred_element_type=F32)

    a_hi, b_hi = a.astype(BF16), b.astype(BF16)
    a_lo, b_lo = (a - a_hi.astype(F32)).astype(BF16), (b - b_hi.astype(F32)).astype(BF16)
    return dot(a_hi, b_hi) + (dot(a_hi, b_lo) + dot(a_lo, b_hi))


def iota(shape, dim):
    return lax.broadcasted_iota(jnp.int32, shape, dim)


def kernel(
    hid, grads, mom, wts, ids, counts, consts,
    out, mom_out,
    gath, rows_f, hid_v, gbuf, mom_v, wts_v, ids_v, counts_v, consts_v,
    part, prx, wsum, zbuf, slab, acc_y, acc_x,
    st_y1, rx_y1, st_x1, rx_x1, st_y2, rx_y2, st_x2, rx_x2,
    load_sem, in_sem, pair_s, pair_r,
    y1_s, y1_r, x1_s, x1_r, y2_s, y2_r, x2_s, x2_r,
    z_s, z_r, gy_s, gy_r, gx_s, gx_r, ry_s, ry_r, rx_s, rx_r, fw_s, fw_r,
):
    shard, z = lax.axis_index("shard"), lax.axis_index("rep")
    c = shard % 2
    y = (shard // 2) % NY
    x = shard // (2 * NY)

    def dev(xx, yy, cc):
        return ((xx * NY + yy) * 2 + cc, z)

    def y_at(d):
        return (y + d) % NY

    def x_at(d):
        return (x + d) % NX

    def to_y(d):
        return dev(x, y_at(d), c)

    def to_x(d):
        return dev(x_at(d), y, c)

    def remote(src, dst, send, recv, who):
        return pltpu.make_async_remote_copy(
            src_ref=src, dst_ref=dst, send_sem=send, recv_sem=recv,
            device_id=who, device_id_type=MESH,
        )

    pair = dev(x, y, 1 - c)
    barrier = pltpu.get_barrier_semaphore()
    partners = [pair] + [to_x(d) for d in X_FAR] + [to_y(d) for d in Y_FAR]
    partners += [(shard, (z + d) % NZ) for d in range(1, NZ)]
    for who in partners:
        pl.semaphore_signal(barrier, inc=1, device_id=who, device_id_type=MESH)

    moves = []
    for k, (src, dst) in enumerate((
        (hid.at[0], hid_v), (mom, mom_v), (wts, wts_v), (ids, ids_v), (counts, counts_v),
        (consts, consts_v),
    )):
        moves.append(pltpu.make_async_copy(src, dst, in_sem.at[k]))
    moves[0].start()
    loads = []
    for p in range(PARTS):
        cp = pltpu.make_async_copy(
            grads.at[0, :, pl.ds(p * PART_COLS, PART_COLS)], gbuf.at[p], load_sem.at[p]
        )
        cp.start()
        loads.append(cp)
    for cp in moves[1:]:
        cp.start()
    moves[0].wait()

    r_, c_ = iota((128, 128), 0), iota((128, 128), 1)
    src = (r_ // 64) * 64 + (r_ % 32) * 2 + (r_ % 64) // 32
    perm = jnp.where(c_ == src, 1.0, 0.0).astype(BF16)
    hid_t = lax.dot_general(
        perm, hid_v[...], (((1,), (1,)), ((), ())), preferred_element_type=F32
    ).astype(BF16)

    left = iota((32, 128), 1) < 64
    for p in range(PARTS):
        loads[p].wait()
        full = jnp.dot(hid_t, gbuf[p], preferred_element_type=F32)
        for i in range(2):
            for q in range(PART_CHIPS):
                chip = i * 16 + p * PART_CHIPS + q
                for b in range(3):
                    cols = slice(q * 384 + b * 128, q * 384 + (b + 1) * 128)
                    ev = full[i * 64:i * 64 + 32, cols]
                    od = full[i * 64 + 32:i * 64 + 64, cols]
                    first = jnp.where(left, ev, pltpu.roll(od, 64, 1)).astype(BF16)
                    second = jnp.where(left, pltpu.roll(ev, 64, 1), od).astype(BF16)
                    for t, val in ((2 * b, first), (2 * b + 1, second)):
                        row = (t % 3) * 32
                        part[t // 3, chip // 8, chip % 8, row:row + 32, :] = val
    pl.semaphore_wait(barrier, len(partners))

    ys, xs = slice(0, Y_ROWS), slice(Y_ROWS, ROWS)
    every = slice(None)
    y_rows, x_rows = pl.ds(0, Y_ROWS), pl.ds(Y_ROWS, ROWS - Y_ROWS)
    pair_copies = []
    for k, ix in enumerate(
        [(x_at(d), every, x_rows) for d in X_FAR] + [(every, every, y_rows), (x, every, x_rows)]
    ):
        cp = remote(part.at[(1 - c,) + ix], prx.at[ix], pair_s.at[k], pair_r.at[k], pair)
        cp.start()
        pair_copies.append(cp)

    def own(ix):
        return part[(c,) + ix] + prx[ix]

    first_x, first_y, second_y, second_x = [], [], [], []
    order = Y_FAR + (0,)
    step = NY // X_PARTS
    for part_no in range(X_PARTS):
        ks = range(part_no * step, (part_no + 1) * step)
        for i, d in enumerate(X_FAR):
            if part_no == 0:
                pair_copies[i].wait_recv()
            for k in ks:
                st_x1[d - 1, k] = own((x_at(d), y_at(order[k]), xs))
            at = pl.ds(part_no * step, step)
            n = (d - 1) * X_PARTS + part_no
            cp = remote(st_x1.at[d - 1, at], rx_x1.at[d - 1, at], x1_s.at[n], x1_r.at[n], to_x(d))
            cp.start()
            first_x.append(cp)
        if part_no == 0:
            pair_copies[3].wait_recv()
            for d in Y_FAR:
                st_y1[d - 1] = own((every, y_at(d), ys))
                cp = remote(st_y1.at[d - 1], rx_y1.at[d - 1], y1_s.at[d - 1], y1_r.at[d - 1], to_y(d))
                cp.start()
                first_y.append(cp)
    pair_copies[4].wait_recv()
    for part_no in range(X_PARTS):
        for cp in first_x[3 * part_no:3 * part_no + 3]:
            cp.wait_recv()
        for k in range(part_no * step, (part_no + 1) * step):
            total = own((x, y_at(order[k]), xs)).astype(F32)
            for d in X_FAR:
                total = total + rx_x1[d - 1, k].astype(F32)
            d = order[k]
            if d == 0:
                acc_x[...] = total
                continue
            st_y2[d - 1] = total.astype(BF16)
            cp = remote(st_y2.at[d - 1], rx_y2.at[d - 1], y2_s.at[d - 1], y2_r.at[d - 1], to_y(d))
            cp.start()
            second_y.append(cp)
    total = own((every, y, ys)).astype(F32)
    for cp, d in zip(first_y, Y_FAR):
        cp.wait_recv()
        total = total + rx_y1[d - 1].astype(F32)
    acc_y[...] = total
    for d in X_FAR:
        st_x2[d - 1] = acc_y[x_at(d)].astype(BF16)
        cp = remote(st_x2.at[d - 1], rx_x2.at[d - 1], x2_s.at[d - 1], x2_r.at[d - 1], to_x(d))
        cp.start()
        second_x.append(cp)
    total = acc_x[...]
    for cp, d in zip(second_y, Y_FAR):
        cp.wait_recv()
        total = total + rx_y2[d - 1].astype(F32)
    slab[xs] = total
    total = acc_y[x]
    for cp, d in zip(second_x, X_FAR):
        cp.wait_recv()
        total = total + rx_x2[d - 1].astype(F32)
    slab[ys] = total
    for cp in moves[1:]:
        cp.wait()

    moment = MOMENTUM_DECAY * mom_v[...] + GRAD_SCALE * slab[...]
    both, diag = consts_v[0:128], consts_v[128:256]
    fwd, inv = consts_v[256:384, 0:32], consts_v[384:448, 0:64]
    tiles = jnp.concatenate([moment[0:32], moment[32:64], moment[64:96]], axis=1)
    v = dot32(fwd, tiles)
    left64 = iota((64, 128), 1) < 64
    v = jnp.concatenate(
        [
            jnp.where(left64, v[0:64, k * 128:(k + 1) * 128], v[64:128, k * 128:(k + 1) * 128])
            for k in range(3)
        ],
        axis=0,
    )
    coef = dot32(v, both)

    group = (iota((64, 128), 1) % 64) // 16
    unit = (iota((64, 128), 0) // 8) * 4 + group
    kept = []
    for k in range(3):
        keep = jnp.zeros((64, 128), F32)
        for j in range(4):
            live = jnp.where(j < counts_v[0, k], ids_v[k, 0, j], -1)
            keep = jnp.where(unit == live, 1.0, keep)
        kept.append(coef[k * 64:(k + 1) * 64] * keep)

    lane8 = iota((8, 128), 1)
    row8 = iota((8, 128), 0)
    picked = []
    numbers = jnp.zeros((8, 128), F32)
    for k in range(3):
        for j in range(4):
            number = ids_v[k, 0, j]
            block = jnp.zeros((8, 128), F32)
            for p in range(8):
                block = jnp.where(number // 4 == p, kept[k][p * 8:(p + 1) * 8], block)
            here = (lane8 // 16) == number % 4
            picked.append(jnp.where(here & (j < counts_v[0, k]), block, 0.0))
            slot = (row8 == k) & (lane8 // 16 == 4 + j)
            numbers = jnp.where(slot, number.astype(F32), numbers)
    picked = jnp.concatenate(picked, axis=0).astype(BF16)
    spread = jnp.where(
        iota((128, 128), 0) % 16 == iota((128, 128), 1) % 16, 1.0, 0.0
    ).astype(BF16)
    picked = jnp.dot(picked, spread, preferred_element_type=F32)
    halves = [jnp.zeros((8, 128), F32), numbers]
    for k in range(3):
        for j in range(4):
            at = (k * 4 + j) * 8
            halves[k // 2] = jnp.where(
                lane8 // 16 == (k % 2) * 4 + j, picked[at:at + 8], halves[k // 2]
            )
    zbuf[z] = jnp.concatenate(halves, axis=0).astype(BF16)
    sends = []
    for d in range(1, NZ):
        cp = pltpu.make_async_remote_copy(
            src_ref=zbuf.at[z], dst_ref=zbuf.at[z],
            send_sem=z_s.at[d - 1], recv_sem=z_r.at[d - 1],
            device_id=(shard, (z + d) % NZ), device_id_type=MESH,
        )
        cp.start()
        sends.append(cp)

    def inverse(rows):
        kb = dot32(rows, diag)
        kb = jnp.concatenate([kb[0:64], kb[64:128], kb[128:192]], axis=1)
        w = dot32(inv, kb)
        return jnp.concatenate(
            [
                jnp.where(left, w[0:32, k * 128:(k + 1) * 128], w[32:64, k * 128:(k + 1) * 128])
                for k in range(3)
            ],
            axis=0,
        )

    mom_out[...] = moment - inverse(jnp.concatenate(kept, axis=0))
    for m in range(32):
        wsum[pl.ds(m, 3, stride=32), :] = wts_v[:, m * 128:(m + 1) * 128].astype(F32)

    for d in range(1, NZ):
        frm = (z + NZ - d) % NZ
        pltpu.make_async_remote_copy(
            src_ref=zbuf.at[z], dst_ref=zbuf.at[frm],
            send_sem=z_s.at[d - 1], recv_sem=z_r.at[d - 1],
            device_id=(shard, frm), device_id_type=MESH,
        ).wait_recv()

    wide = iota((128, 1024), 1)
    pick = (wide // 128 == iota((128, 1024), 0) // 16) & (wide % 16 == iota((128, 1024), 0) % 16)
    pick = jnp.where(pick, 1.0, 0.0).astype(BF16)
    msgs = jnp.concatenate([zbuf[r] for r in range(NZ)], axis=0)
    vals = jnp.dot(msgs, pick, preferred_element_type=F32)
    unitf = unit.astype(F32)
    totals = []
    for k in range(3):
        total = jnp.zeros((64, 128), F32)
        for r in range(NZ):
            for j in range(4):
                col = ((k % 2) * 4 + j) * 128
                row = r * 16 + (k // 2) * 8
                val = vals[row:row + 8, col:col + 128]
                num = vals[r * 16 + 8 + k:r * 16 + 9 + k, (4 + j) * 128:(5 + j) * 128]
                val = jnp.concatenate([val] * 8, axis=0)
                total = total + jnp.where(unitf == num, val, 0.0)
        totals.append(total)
    update = inverse(jnp.concatenate(totals, axis=0))
    gath[x, 0, c] = (wsum[...] - STEP * update).astype(BF16)


    sends += pair_copies + first_x + first_y + second_x + second_y
    lower, upper = pl.ds(0, G_ROWS), pl.ds(G_ROWS, ROWS - G_ROWS)

    def go(src, dst, send, recv, who):
        cp = remote(src, dst, send, recv, who)
        cp.start()
        sends.append(cp)

    def got(dst, send, recv):
        remote(dst, dst, send, recv, pair).wait_recv()

    def place(cc, i, k):
        tile = ((i * NY + y_at(NY - OFFSETS[k])) * 2 + cc) * 3
        val = gath[i, k, cc].astype(F32)
        for t in range(3):
            rows_f[pl.ds(tile + t, 32, stride=192), :] = val[t * 32:(t + 1) * 32]

    def slabs(cc, lo, hi):
        return gath.at[:, pl.ds(lo, hi - lo), cc]

    for d in X_FAR:
        mine = gath.at[x, 0, c]
        go(mine, mine, gx_s.at[d - 1], gx_r.at[d - 1], to_x(d))
    for k in range(1, NY):
        go(
            gath.at[x, 0, c, upper], gath.at[x, k, c, upper], gy_s.at[k - 1], gy_r.at[k - 1],
            to_y(OFFSETS[k]),
        )
    for d in X_FAR:
        got(gath.at[x_at(NX - d), 0, c], gx_s.at[d - 1], gx_r.at[d - 1])
    for k in range(1, NY):
        go(
            gath.at[:, 0, c, lower], gath.at[:, k, c, lower], ry_s.at[k - 1], ry_r.at[k - 1],
            to_y(OFFSETS[k]),
        )
    go(slabs(c, 0, 1), slabs(c, 0, 1), fw_s.at[0], fw_r.at[0], pair)
    for i in range(NX):
        place(c, i, 0)
    for n, (lo, hi) in enumerate(K_GROUPS):
        for k in range(lo, hi):
            got(gath.at[x, k, c, upper], gy_s.at[k - 1], gy_r.at[k - 1])
        for d in X_FAR:
            ref = gath.at[x, pl.ds(lo, hi - lo), c, upper]
            m = n * 3 + d - 1
            go(ref, ref, rx_s.at[m], rx_r.at[m], to_x(d))
    got(slabs(1 - c, 0, 1), fw_s.at[0], fw_r.at[0])
    for i in range(NX):
        place(1 - c, i, 0)
    for n, (lo, hi) in enumerate(K_GROUPS):
        for k in range(lo, hi):
            got(gath.at[:, k, c, lower], ry_s.at[k - 1], ry_r.at[k - 1])
        for d in X_FAR:
            m = n * 3 + d - 1
            got(gath.at[x_at(NX - d), pl.ds(lo, hi - lo), c, upper], rx_s.at[m], rx_r.at[m])
        go(slabs(c, lo, hi), slabs(c, lo, hi), fw_s.at[n + 1], fw_r.at[n + 1], pair)
        for k in range(lo, hi):
            for i in range(NX):
                place(c, i, k)
    for n, (lo, hi) in enumerate(K_GROUPS):
        got(slabs(1 - c, lo, hi), fw_s.at[n + 1], fw_r.at[n + 1])
        for k in range(lo, hi):
            for i in range(NX):
                place(1 - c, i, k)
    for m in range(32):
        out[:, m * 128:(m + 1) * 128] = rows_f[m * 192:(m + 1) * 192].astype(BF16)
    for cp in sends:
        cp.wait_send()


def body(hidden_acts, out_grads, momentum, weight_tiles, kept_ids, kept_counts):
    hbm = pl.BlockSpec(memory_space=pltpu.HBM)
    vmem = pl.BlockSpec(memory_space=pltpu.VMEM)

    def both(*shape):
        return [pltpu.VMEM(shape, BF16)] * 2

    def pairs(*counts):
        return [pltpu.SemaphoreType.DMA((n,)) for n in counts for _ in range(2)]

    dma = pltpu.SemaphoreType.DMA
    gathered, moment_out = pl.pallas_call(
        kernel,
        out_shape=(
            jax.ShapeDtypeStruct((192, TILE_SQ), BF16),
            jax.ShapeDtypeStruct((ROWS, 128), F32),
        ),
        in_specs=[hbm] * 7,
        out_specs=(vmem, vmem),
        scratch_shapes=[
            pltpu.VMEM((NX, NY, 2, ROWS, 128), BF16),
            pltpu.VMEM((32 * 192, 128), F32),
            pltpu.VMEM((256, 128), BF16),
            pltpu.VMEM((PARTS, 256, PART_COLS), BF16),
            pltpu.VMEM((ROWS, 128), F32),
            pltpu.VMEM((3, TILE_SQ), BF16),
            pltpu.SMEM((3, 1, 4), jnp.int32),
            pltpu.SMEM((1, 3), jnp.int32),
            pltpu.VMEM((448, 128), F32),
            pltpu.VMEM((2, NX, NY, ROWS, 128), BF16),
            pltpu.VMEM((NX, NY, ROWS, 128), BF16),
            pltpu.VMEM((ROWS, 128), F32),
            pltpu.VMEM((NZ, 16, 128), BF16),
            pltpu.VMEM((ROWS, 128), F32),
            pltpu.VMEM((NX, Y_ROWS, 128), F32),
            pltpu.VMEM((ROWS - Y_ROWS, 128), F32),
            *both(NY - 1, NX, Y_ROWS, 128),
            *both(NX - 1, NY, ROWS - Y_ROWS, 128),
            *both(NY - 1, ROWS - Y_ROWS, 128),
            *both(NX - 1, Y_ROWS, 128),
            dma((PARTS,)),
            dma((6,)),
            *pairs(5, 7, 3 * X_PARTS, 7, 3, 7, 7, 3, 7, 3 * len(K_GROUPS), 1 + len(K_GROUPS)),
        ],
        compiler_params=pltpu.CompilerParams(
            collective_id=0, has_side_effects=True, vmem_limit_bytes=48 * 1024 * 1024
        ),
    )(*(
        pltpu.with_memory_space_constraint(arg, pltpu.HBM)
        for arg in (
            hidden_acts, out_grads, momentum.reshape(ROWS, 128), weight_tiles,
            kept_ids.transpose(1, 0, 2), kept_counts, jnp.asarray(constants()),
        )
    ))
    return gathered, moment_out.reshape(1, 3, TILE_SQ)


def solution(mesh):
    in_specs = (
        P("rep", "shard", None),
        P("rep", "shard", None),
        P("rep", "shard", None),
        P("shard", None),
        P("rep", "shard", None),
        P("rep", "shard"),
    )
    out_specs = (P(), P("rep", "shard", None))
    return jax.shard_map(body, mesh=mesh, in_specs=in_specs, out_specs=out_specs, check_vma=False)
```

```python
import math

import jax
import jax.numpy as jnp
import numpy as np
from jax import lax
from jax.experimental import pallas as pl
from jax.experimental.pallas import tpu as pltpu
from jax.sharding import PartitionSpec as P

TILE = 64
BLOCKS = 32
TILE_SQ = 4096
D = 6144
NX, NY, NZ = 4, 8, 8
ROWS = 96
Y_ROWS = 32
G_ROWS = 32
X_FAR = (2, 1, 3)
Y_FAR = (4, 3, 5, 2, 6, 1, 7)
OFFSETS = (0,) + Y_FAR
K_GROUPS = ((1, 3), (3, 5), (5, 8))
X_PARTS = 2
PARTS = 4
PART_COLS = D // PARTS
PART_CHIPS = PART_COLS // 384
MOMENTUM_DECAY = 0.9
STEP = 2.0 / 8.0
GRAD_SCALE = 1.0 / 128.0
MESH = pl.DeviceIdType.MESH
F32 = jnp.float32
BF16 = jnp.bfloat16


def constants():
    k = np.arange(TILE, dtype=np.float64)[:, None]
    n = np.arange(TILE, dtype=np.float64)[None, :]
    basis = np.cos(math.pi * (2 * n + 1) * k / (2 * TILE))
    basis *= np.where(k == 0, math.sqrt(1 / TILE), math.sqrt(2 / TILE))
    even, odd = basis[:, 0::2], basis[:, 1::2]
    out = np.zeros((448, 128))
    out[0:128] = np.tile(basis.T, (2, 2))
    out[128:192, 0:64] = basis
    out[192:256, 64:128] = basis
    out[256:384, 0:32] = np.concatenate([even, odd], 0)
    out[384:448, 0:64] = np.concatenate([even.T, odd.T], 0)
    return out.astype(np.float32)


def dot32(a, b):
    def dot(u, v):
        return jnp.dot(u, v, preferred_element_type=F32)

    a_hi, b_hi = a.astype(BF16), b.astype(BF16)
    a_lo, b_lo = (a - a_hi.astype(F32)).astype(BF16), (b - b_hi.astype(F32)).astype(BF16)
    return dot(a_hi, b_hi) + (dot(a_hi, b_lo) + dot(a_lo, b_hi))


def iota(shape, dim):
    return lax.broadcasted_iota(jnp.int32, shape, dim)


def kernel(
    hid, grads, mom, wts, ids, counts, consts,
    out, mom_out,
    gath, rows_f, hid_v, gbuf, mom_v, wts_v, ids_v, counts_v, consts_v,
    part, prx, wsum, zbuf, slab, acc_y, acc_x,
    st_y1, rx_y1, st_x1, rx_x1, st_y2, rx_y2, st_x2, rx_x2,
    load_sem, in_sem, pair_s, pair_r,
    y1_s, y1_r, x1_s, x1_r, y2_s, y2_r, x2_s, x2_r,
    z_s, z_r, gy_s, gy_r, gx_s, gx_r, ry_s, ry_r, rx_s, rx_r, fw_s, fw_r,
):
    shard, z = lax.axis_index("shard"), lax.axis_index("rep")
    c = shard % 2
    y = (shard // 2) % NY
    x = shard // (2 * NY)

    def dev(xx, yy, cc):
        return ((xx * NY + yy) * 2 + cc, z)

    def y_at(d):
        return (y + d) % NY

    def x_at(d):
        return (x + d) % NX

    def to_y(d):
        return dev(x, y_at(d), c)

    def to_x(d):
        return dev(x_at(d), y, c)

    def remote(src, dst, send, recv, who):
        return pltpu.make_async_remote_copy(
            src_ref=src, dst_ref=dst, send_sem=send, recv_sem=recv,
            device_id=who, device_id_type=MESH,
        )

    pair = dev(x, y, 1 - c)
    barrier = pltpu.get_barrier_semaphore()
    partners = [pair] + [to_x(d) for d in X_FAR] + [to_y(d) for d in Y_FAR]
    partners += [(shard, (z + d) % NZ) for d in range(1, NZ)]
    for who in partners:
        pl.semaphore_signal(barrier, inc=1, device_id=who, device_id_type=MESH)

    moves = []
    for k, (src, dst) in enumerate((
        (hid.at[0], hid_v), (mom, mom_v), (wts, wts_v), (ids, ids_v), (counts, counts_v),
        (consts, consts_v),
    )):
        moves.append(pltpu.make_async_copy(src, dst, in_sem.at[k]))
    moves[0].start()
    loads = []
    for p in range(PARTS):
        cp = pltpu.make_async_copy(
            grads.at[0, :, pl.ds(p * PART_COLS, PART_COLS)], gbuf.at[p], load_sem.at[p]
        )
        cp.start()
        loads.append(cp)
    for cp in moves[1:]:
        cp.start()
    moves[0].wait()

    r_, c_ = iota((128, 128), 0), iota((128, 128), 1)
    src = (r_ // 64) * 64 + (r_ % 32) * 2 + (r_ % 64) // 32
    perm = jnp.where(c_ == src, 1.0, 0.0).astype(BF16)
    hid_t = lax.dot_general(
        perm, hid_v[...], (((1,), (1,)), ((), ())), preferred_element_type=F32
    ).astype(BF16)

    left = iota((32, 128), 1) < 64
    for p in range(PARTS):
        loads[p].wait()
        full = jnp.dot(hid_t, gbuf[p], preferred_element_type=F32)
        for i in range(2):
            for q in range(PART_CHIPS):
                chip = i * 16 + p * PART_CHIPS + q
                for b in range(3):
                    cols = slice(q * 384 + b * 128, q * 384 + (b + 1) * 128)
                    ev = full[i * 64:i * 64 + 32, cols]
                    od = full[i * 64 + 32:i * 64 + 64, cols]
                    first = jnp.where(left, ev, pltpu.roll(od, 64, 1)).astype(BF16)
                    second = jnp.where(left, pltpu.roll(ev, 64, 1), od).astype(BF16)
                    for t, val in ((2 * b, first), (2 * b + 1, second)):
                        row = (t % 3) * 32
                        part[t // 3, chip // 8, chip % 8, row:row + 32, :] = val
    pl.semaphore_wait(barrier, len(partners))

    ys, xs = slice(0, Y_ROWS), slice(Y_ROWS, ROWS)
    every = slice(None)
    y_rows, x_rows = pl.ds(0, Y_ROWS), pl.ds(Y_ROWS, ROWS - Y_ROWS)
    pair_copies = []
    for k, ix in enumerate(
        [(x_at(d), every, x_rows) for d in X_FAR] + [(every, every, y_rows), (x, every, x_rows)]
    ):
        cp = remote(part.at[(1 - c,) + ix], prx.at[ix], pair_s.at[k], pair_r.at[k], pair)
        cp.start()
        pair_copies.append(cp)

    def own(ix):
        return part[(c,) + ix] + prx[ix]

    first_x, first_y, second_y, second_x = [], [], [], []
    order = Y_FAR + (0,)
    step = NY // X_PARTS
    for part_no in range(X_PARTS):
        ks = range(part_no * step, (part_no + 1) * step)
        for i, d in enumerate(X_FAR):
            if part_no == 0:
                pair_copies[i].wait_recv()
            for k in ks:
                st_x1[d - 1, k] = own((x_at(d), y_at(order[k]), xs))
            at = pl.ds(part_no * step, step)
            n = (d - 1) * X_PARTS + part_no
            cp = remote(st_x1.at[d - 1, at], rx_x1.at[d - 1, at], x1_s.at[n], x1_r.at[n], to_x(d))
            cp.start()
            first_x.append(cp)
        if part_no == 0:
            pair_copies[3].wait_recv()
            for d in Y_FAR:
                st_y1[d - 1] = own((every, y_at(d), ys))
                cp = remote(st_y1.at[d - 1], rx_y1.at[d - 1], y1_s.at[d - 1], y1_r.at[d - 1], to_y(d))
                cp.start()
                first_y.append(cp)
    pair_copies[4].wait_recv()
    for part_no in range(X_PARTS):
        for cp in first_x[3 * part_no:3 * part_no + 3]:
            cp.wait_recv()
        for k in range(part_no * step, (part_no + 1) * step):
            total = own((x, y_at(order[k]), xs)).astype(F32)
            for d in X_FAR:
                total = total + rx_x1[d - 1, k].astype(F32)
            d = order[k]
            if d == 0:
                acc_x[...] = total
                continue
            st_y2[d - 1] = total.astype(BF16)
            cp = remote(st_y2.at[d - 1], rx_y2.at[d - 1], y2_s.at[d - 1], y2_r.at[d - 1], to_y(d))
            cp.start()
            second_y.append(cp)
    total = own((every, y, ys)).astype(F32)
    for cp, d in zip(first_y, Y_FAR):
        cp.wait_recv()
        total = total + rx_y1[d - 1].astype(F32)
    acc_y[...] = total
    for d in X_FAR:
        st_x2[d - 1] = acc_y[x_at(d)].astype(BF16)
        cp = remote(st_x2.at[d - 1], rx_x2.at[d - 1], x2_s.at[d - 1], x2_r.at[d - 1], to_x(d))
        cp.start()
        second_x.append(cp)
    total = acc_x[...]
    for cp, d in zip(second_y, Y_FAR):
        cp.wait_recv()
        total = total + rx_y2[d - 1].astype(F32)
    slab[xs] = total
    total = acc_y[x]
    for cp, d in zip(second_x, X_FAR):
        cp.wait_recv()
        total = total + rx_x2[d - 1].astype(F32)
    slab[ys] = total
    for cp in moves[1:]:
        cp.wait()

    moment = MOMENTUM_DECAY * mom_v[...] + GRAD_SCALE * slab[...]
    both, diag = consts_v[0:128], consts_v[128:256]
    fwd, inv = consts_v[256:384, 0:32], consts_v[384:448, 0:64]
    tiles = jnp.concatenate([moment[0:32], moment[32:64], moment[64:96]], axis=1)
    v = dot32(fwd, tiles)
    left64 = iota((64, 128), 1) < 64
    v = jnp.concatenate(
        [
            jnp.where(left64, v[0:64, k * 128:(k + 1) * 128], v[64:128, k * 128:(k + 1) * 128])
            for k in range(3)
        ],
        axis=0,
    )
    coef = dot32(v, both)

    group = (iota((64, 128), 1) % 64) // 16
    unit = (iota((64, 128), 0) // 8) * 4 + group
    kept = []
    for k in range(3):
        keep = jnp.zeros((64, 128), F32)
        for j in range(4):
            live = jnp.where(j < counts_v[0, k], ids_v[k, 0, j], -1)
            keep = jnp.where(unit == live, 1.0, keep)
        kept.append(coef[k * 64:(k + 1) * 64] * keep)

    lane8 = iota((8, 128), 1)
    row8 = iota((8, 128), 0)
    picked = []
    numbers = jnp.zeros((8, 128), F32)
    for k in range(3):
        for j in range(4):
            number = ids_v[k, 0, j]
            block = jnp.zeros((8, 128), F32)
            for p in range(8):
                block = jnp.where(number // 4 == p, kept[k][p * 8:(p + 1) * 8], block)
            here = (lane8 // 16) == number % 4
            picked.append(jnp.where(here & (j < counts_v[0, k]), block, 0.0))
            slot = (row8 == k) & (lane8 // 16 == 4 + j)
            numbers = jnp.where(slot, number.astype(F32), numbers)
    picked = jnp.concatenate(picked, axis=0).astype(BF16)
    spread = jnp.where(
        iota((128, 128), 0) % 16 == iota((128, 128), 1) % 16, 1.0, 0.0
    ).astype(BF16)
    picked = jnp.dot(picked, spread, preferred_element_type=F32)
    halves = [jnp.zeros((8, 128), F32), numbers]
    for k in range(3):
        for j in range(4):
            at = (k * 4 + j) * 8
            halves[k // 2] = jnp.where(
                lane8 // 16 == (k % 2) * 4 + j, picked[at:at + 8], halves[k // 2]
            )
    zbuf[z] = jnp.concatenate(halves, axis=0).astype(BF16)
    sends = []
    for d in range(1, NZ):
        cp = pltpu.make_async_remote_copy(
            src_ref=zbuf.at[z], dst_ref=zbuf.at[z],
            send_sem=z_s.at[d - 1], recv_sem=z_r.at[d - 1],
            device_id=(shard, (z + d) % NZ), device_id_type=MESH,
        )
        cp.start()
        sends.append(cp)

    def inverse(rows):
        kb = dot32(rows, diag)
        kb = jnp.concatenate([kb[0:64], kb[64:128], kb[128:192]], axis=1)
        w = dot32(inv, kb)
        return jnp.concatenate(
            [
                jnp.where(left, w[0:32, k * 128:(k + 1) * 128], w[32:64, k * 128:(k + 1) * 128])
                for k in range(3)
            ],
            axis=0,
        )

    mom_out[...] = moment - inverse(jnp.concatenate(kept, axis=0))
    for m in range(32):
        wsum[pl.ds(m, 3, stride=32), :] = wts_v[:, m * 128:(m + 1) * 128].astype(F32)

    for d in range(1, NZ):
        frm = (z + NZ - d) % NZ
        pltpu.make_async_remote_copy(
            src_ref=zbuf.at[z], dst_ref=zbuf.at[frm],
            send_sem=z_s.at[d - 1], recv_sem=z_r.at[d - 1],
            device_id=(shard, frm), device_id_type=MESH,
        ).wait_recv()

    wide = iota((128, 1024), 1)
    pick = (wide // 128 == iota((128, 1024), 0) // 16) & (wide % 16 == iota((128, 1024), 0) % 16)
    pick = jnp.where(pick, 1.0, 0.0).astype(BF16)
    msgs = jnp.concatenate([zbuf[r] for r in range(NZ)], axis=0)
    vals = jnp.dot(msgs, pick, preferred_element_type=F32)
    unitf = unit.astype(F32)
    totals = []
    for k in range(3):
        total = jnp.zeros((64, 128), F32)
        for r in range(NZ):
            for j in range(4):
                col = ((k % 2) * 4 + j) * 128
                row = r * 16 + (k // 2) * 8
                val = vals[row:row + 8, col:col + 128]
                num = vals[r * 16 + 8 + k:r * 16 + 9 + k, (4 + j) * 128:(5 + j) * 128]
                val = jnp.concatenate([val] * 8, axis=0)
                total = total + jnp.where(unitf == num, val, 0.0)
        totals.append(total)
    update = inverse(jnp.concatenate(totals, axis=0))
    gath[x, 0, c] = (wsum[...] - STEP * update).astype(BF16)


    early = sends + pair_copies + first_x + first_y + second_x + second_y
    sends = []
    lower, upper = pl.ds(0, G_ROWS), pl.ds(G_ROWS, ROWS - G_ROWS)

    def go(src, dst, send, recv, who):
        cp = remote(src, dst, send, recv, who)
        cp.start()
        sends.append(cp)

    def got(dst, send, recv):
        remote(dst, dst, send, recv, pair).wait_recv()

    def place(cc, i, k):
        tile = ((i * NY + y_at(NY - OFFSETS[k])) * 2 + cc) * 3
        val = gath[i, k, cc].astype(F32)
        for t in range(3):
            rows_f[pl.ds(tile + t, 32, stride=192), :] = val[t * 32:(t + 1) * 32]

    def slabs(cc, lo, hi):
        return gath.at[:, pl.ds(lo, hi - lo), cc]

    for d in X_FAR:
        mine = gath.at[x, 0, c]
        go(mine, mine, gx_s.at[d - 1], gx_r.at[d - 1], to_x(d))
    for k in range(1, NY):
        go(
            gath.at[x, 0, c, upper], gath.at[x, k, c, upper], gy_s.at[k - 1], gy_r.at[k - 1],
            to_y(OFFSETS[k]),
        )
    for cp in early:
        cp.wait_send()
    for d in X_FAR:
        got(gath.at[x_at(NX - d), 0, c], gx_s.at[d - 1], gx_r.at[d - 1])
    for k in range(1, NY):
        go(
            gath.at[:, 0, c, lower], gath.at[:, k, c, lower], ry_s.at[k - 1], ry_r.at[k - 1],
            to_y(OFFSETS[k]),
        )
    go(slabs(c, 0, 1), slabs(c, 0, 1), fw_s.at[0], fw_r.at[0], pair)
    for i in range(NX):
        place(c, i, 0)
    for n, (lo, hi) in enumerate(K_GROUPS):
        for k in range(lo, hi):
            got(gath.at[x, k, c, upper], gy_s.at[k - 1], gy_r.at[k - 1])
        for d in X_FAR:
            ref = gath.at[x, pl.ds(lo, hi - lo), c, upper]
            m = n * 3 + d - 1
            go(ref, ref, rx_s.at[m], rx_r.at[m], to_x(d))
    got(slabs(1 - c, 0, 1), fw_s.at[0], fw_r.at[0])
    for i in range(NX):
        place(1 - c, i, 0)
    for n, (lo, hi) in enumerate(K_GROUPS):
        for k in range(lo, hi):
            got(gath.at[:, k, c, lower], ry_s.at[k - 1], ry_r.at[k - 1])
        for d in X_FAR:
            m = n * 3 + d - 1
            got(gath.at[x_at(NX - d), pl.ds(lo, hi - lo), c, upper], rx_s.at[m], rx_r.at[m])
        go(slabs(c, lo, hi), slabs(c, lo, hi), fw_s.at[n + 1], fw_r.at[n + 1], pair)
        for k in range(lo, hi):
            for i in range(NX):
                place(c, i, k)
    for n, (lo, hi) in enumerate(K_GROUPS):
        got(slabs(1 - c, lo, hi), fw_s.at[n + 1], fw_r.at[n + 1])
        for k in range(lo, hi):
            for i in range(NX):
                place(1 - c, i, k)
    for m in range(32):
        out[:, m * 128:(m + 1) * 128] = rows_f[m * 192:(m + 1) * 192].astype(BF16)
    for cp in sends:
        cp.wait_send()


def body(hidden_acts, out_grads, momentum, weight_tiles, kept_ids, kept_counts):
    hbm = pl.BlockSpec(memory_space=pltpu.HBM)
    vmem = pl.BlockSpec(memory_space=pltpu.VMEM)

    def both(*shape):
        return [pltpu.VMEM(shape, BF16)] * 2

    def pairs(*counts):
        return [pltpu.SemaphoreType.DMA((n,)) for n in counts for _ in range(2)]

    dma = pltpu.SemaphoreType.DMA
    gathered, moment_out = pl.pallas_call(
        kernel,
        out_shape=(
            jax.ShapeDtypeStruct((192, TILE_SQ), BF16),
            jax.ShapeDtypeStruct((ROWS, 128), F32),
        ),
        in_specs=[hbm] * 7,
        out_specs=(vmem, vmem),
        scratch_shapes=[
            pltpu.VMEM((NX, NY, 2, ROWS, 128), BF16),
            pltpu.VMEM((32 * 192, 128), F32),
            pltpu.VMEM((256, 128), BF16),
            pltpu.VMEM((PARTS, 256, PART_COLS), BF16),
            pltpu.VMEM((ROWS, 128), F32),
            pltpu.VMEM((3, TILE_SQ), BF16),
            pltpu.SMEM((3, 1, 4), jnp.int32),
            pltpu.SMEM((1, 3), jnp.int32),
            pltpu.VMEM((448, 128), F32),
            pltpu.VMEM((2, NX, NY, ROWS, 128), BF16),
            pltpu.VMEM((NX, NY, ROWS, 128), BF16),
            pltpu.VMEM((ROWS, 128), F32),
            pltpu.VMEM((NZ, 16, 128), BF16),
            pltpu.VMEM((ROWS, 128), F32),
            pltpu.VMEM((NX, Y_ROWS, 128), F32),
            pltpu.VMEM((ROWS - Y_ROWS, 128), F32),
            *both(NY - 1, NX, Y_ROWS, 128),
            *both(NX - 1, NY, ROWS - Y_ROWS, 128),
            *both(NY - 1, ROWS - Y_ROWS, 128),
            *both(NX - 1, Y_ROWS, 128),
            dma((PARTS,)),
            dma((6,)),
            *pairs(5, 7, 3 * X_PARTS, 7, 3, 7, 7, 3, 7, 3 * len(K_GROUPS), 1 + len(K_GROUPS)),
        ],
        compiler_params=pltpu.CompilerParams(
            collective_id=0, has_side_effects=True, vmem_limit_bytes=48 * 1024 * 1024
        ),
    )(*(
        pltpu.with_memory_space_constraint(arg, pltpu.HBM)
        for arg in (
            hidden_acts, out_grads, momentum.reshape(ROWS, 128), weight_tiles,
            kept_ids.transpose(1, 0, 2), kept_counts, jnp.asarray(constants()),
        )
    ))
    return gathered, moment_out.reshape(1, 3, TILE_SQ)


def solution(mesh):
    in_specs = (
        P("rep", "shard", None),
        P("rep", "shard", None),
        P("rep", "shard", None),
        P("shard", None),
        P("rep", "shard", None),
        P("rep", "shard"),
    )
    out_specs = (P(), P("rep", "shard", None))
    return jax.shard_map(body, mesh=mesh, in_specs=in_specs, out_specs=out_specs, check_vma=False)
```
